32 devices in a mesh: groups: 2 (over x), tm: 16 (over z, y, core).
Axes of the slice: x: 2, y: 2, z: 4, core: 2. Of those that a mesh axis runs over, the one named last changes fastest.
Arguments:
- generator: float32 [256, 256], replicated, may hold values from -0.09375 to 0.09375
- derivs: float32 [4096, 256], P(('groups', 'tm')), parts along dimension 0, may hold values from 0 to 1, as said below
- forcing: bfloat16 [4096, 256, 64], P(('groups', 'tm')), parts along dimension 0, may hold values from -6 to 6
- inputs: bfloat16 [4096, 256, 64], P(('groups', 'tm')), parts along dimension 0, may hold values from -6 to 6
- terminal: float32 [512, 64], P('groups'), parts along dimension 0, may hold values from -6 to 6
Outputs:
- adjoint: bfloat16 [4096, 256, 64], P(('groups', 'tm')), parts along dimension 0
- weight_grad: float32 [512, 256], P('groups'), parts along dimension 0
The draws below stay inside these ranges and needn't reach their ends.
There are 2 independent parts, one for each index of `groups`. The reference program is written for one: setup_inputs(seed, part) draws one part's arguments, and reference() takes and returns one part's arrays. A program takes and returns all parts, laid end to end along the dimension named above; an argument that names none is the same for every part. Nothing has to cross between parts.
Inputs may be any that keep to these rules, and one draw needn't show every extreme that they name: `derivs`: every entry is positive and at most 1.
All inputs are finite; a program needn't handle non-finite values.
Results may differ from the reference program's by a relative error of at most 0.0029.
Values sent between devices are 32-bit elements; how exact they have to be, the bound alone decides.
No kernel may reach another device: no remote copies, remote signals or barrier semaphores. Data moves between devices by JAX's collectives and lax.ppermute only.
A program may use at most 128 MiB of HBM per device.

```python
import jax
import jax.numpy as jnp
from jax import lax

H = 256
C = 64
E = 256
TERMS = 12
STEPS = 2048


def draw_derivs(key, part):
    key = jax.random.fold_in(key, 11)
    keys = jax.random.split(key, 3)
    share = 0.12
    slow_log = jnp.log(0.5) / STEPS
    fast_log = -1.0 / 40.0
    pick = jax.random.uniform(keys[0], (H,), jnp.float32)
    logarithm_decays = jnp.where(pick < share, fast_log, slow_log)
    coarse_estimate = jax.random.uniform(keys[1], (STEPS, H), jnp.float32, 0.5, 1.5)
    spots = jax.random.randint(keys[2], (2,), 0, STEPS)
    match_count = jnp.any(jnp.arange(STEPS)[:, None] == spots[None, :], axis=1)
    impulse_pulse = jnp.where(match_count, 0.7, 1.0).astype(jnp.float32)
    return (jnp.exp(logarithm_decays[None, :] * coarse_estimate) * impulse_pulse[:, None]).astype(jnp.float32)


def steps_of(rng, dims, cuts, low, largest):
    loudness = 1.0
    for position, shards_of in cuts:
        draws = jax.random.uniform(jax.random.fold_in(jax.random.fold_in(rng, 6), position), (shards_of,), jnp.float32, low / len(cuts), largest / len(cuts))
        loudness = loudness * jnp.repeat(jnp.exp(draws), dims[position] // shards_of).reshape((-1,) + (1,) * (len(dims) - 1 - position))
    return loudness


def bell_draw(stream_key, dims, scale, limit, shards=(), kind=jnp.bfloat16):
    drawn = scale * jax.random.normal(stream_key, dims, jnp.float32)
    if shards:
        drawn = drawn * steps_of(stream_key, dims, shards, -0.22, 0.18)
    return jnp.clip(drawn, -limit, limit).astype(kind)


def setup_inputs(seed: int = 0, part: int = 0) -> dict:
    seeds = jax.random.split(jax.random.key(seed), 6)
    part_splits = jax.random.split(jax.random.fold_in(seeds[5], part), 6)
    return {
        "generator": bell_draw(seeds[0], (H, H), (16 * H) ** -0.5, 0.09375, (), jnp.float32),
        "derivs": draw_derivs(jax.random.fold_in(jax.random.fold_in(seeds[5], part), 71), part),
        "forcing": bell_draw(part_splits[2], (STEPS, H, C), 1.0, 6.0, ((0, 16),)),
        "inputs": bell_draw(part_splits[3], (STEPS, E, C), 1.0, 6.0, ((0, 16),)),
        "terminal": bell_draw(part_splits[4], (H, C), 1.0, 6.0, (), jnp.float32),
    }


def rotation(generator):
    skew = generator - generator.T
    ident = jnp.eye(generator.shape[0], dtype=jnp.float32)
    term = ident
    total = ident
    for order in range(1, TERMS + 1):
        term = jnp.dot(term, skew, precision=lax.Precision.HIGHEST, preferred_element_type=jnp.float32) / float(order)
        total = total + term
    return total


def reference(generator, derivs, forcing, inputs, terminal):
    recur_t = rotation(generator).T

    def forward_move(state, triple):
        deriv, force = triple
        scaled = deriv[:, None] * state
        updated_state = jnp.dot(recur_t, scaled, precision=lax.Precision.HIGHEST, preferred_element_type=jnp.float32) + force.astype(jnp.float32)
        return updated_state, updated_state

    final, states = lax.scan(forward_move, terminal, (derivs, forcing), reverse=True)
    low = states.astype(jnp.bfloat16)
    left = jnp.transpose(low, (1, 0, 2)).reshape(H, STEPS * C)
    right = jnp.transpose(inputs, (1, 0, 2)).reshape(E, STEPS * C)
    weight_grad = jnp.dot(left, right.T, preferred_element_type=jnp.float32)
    return low, weight_grad
```

```python
import math

import jax
import jax.numpy as jnp
from jax import lax
from jax.experimental import pallas as pl
from jax.experimental.pallas import tpu as pltpu
from jax.sharding import PartitionSpec as P

F32 = jnp.float32
BF16 = jnp.bfloat16
VMEM_LIMIT = 56 * 1024 * 1024
CHUNKS = 4
SEG = 8


def mm(a, b):
    return jnp.dot(a, b, preferred_element_type=F32)


def full_mm(a, b):
    return jnp.dot(a, b, precision=lax.Precision.HIGHEST, preferred_element_type=F32)


def split(x):
    high = x.astype(BF16)
    low = (x - high.astype(F32)).astype(BF16)
    return high, low


def mm3(a, b_high, b_low):
    a_high, a_low = split(a)
    return mm(a_high, b_high) + mm(a_low, b_high) + mm(a_high, b_low)


def rotation(gen):
    n = gen.shape[0]
    skew = gen - gen.T
    ident = (
        lax.broadcasted_iota(jnp.int32, (n, n), 0) == lax.broadcasted_iota(jnp.int32, (n, n), 1)
    ).astype(F32)
    c = [1.0 / math.factorial(k) for k in range(13)]
    s2 = full_mm(skew, skew)
    s3 = full_mm(s2, skew)
    s4 = full_mm(s2, s2)
    top = c[8] * ident + c[9] * skew + c[10] * s2 + c[11] * s3 + c[12] * s4
    mid = c[4] * ident + c[5] * skew + c[6] * s2 + c[7] * s3
    bottom = ident + skew + c[2] * s2 + c[3] * s3
    return bottom + full_mm(s4, mid + full_mm(s4, top)), ident


def compose_into(later, high, low, vec, width):
    out = mm3(later, high, low)
    return jnp.concatenate([out[:width], out[width:] + vec], axis=0)


def build_kernel(gen_ref, d_ref, f_ref, map_ref, raw_ref, suffix_ref, rot_ref, state):
    steps, width = d_ref.shape
    per = steps // CHUNKS
    marks = per // SEG
    rot, ident = rotation(gen_ref[...])
    rot_high, rot_low = split(rot)
    rot_ref[0] = rot_high
    rot_ref[1] = rot_low
    for g in range(CHUNKS):
        state[g, :width] = ident
        state[g, width:] = jnp.zeros_like(state[g, width:])

    def step(s, _):
        for g in range(CHUNKS):
            t = g * per + per - 1 - s
            out = mm3(state[g] * d_ref[pl.ds(t, 1), :], rot_ref[0], rot_ref[1])
            state[g, :width] = out[:width]
            state[g, width:] = out[width:] + f_ref[t].astype(F32)
        return 0

    for k in range(marks):
        lax.fori_loop(k * SEG, (k + 1) * SEG, step, 0)
        for g in range(CHUNKS):
            raw_ref[g * marks + marks - 1 - k] = state[g]

    acc = state[CHUNKS - 1]
    for g in range(CHUNKS - 2, -1, -1):
        suffix_ref[g] = acc
        high, low = split(state[g, :width])
        acc = compose_into(acc, high, low, state[g, width:], width)
    map_ref[...] = acc


def marks_kernel(raw_ref, suffix_ref, in_ref, zh_ref, zl_ref, zu_ref, flip_ref):
    count, rows, width = raw_ref.shape
    cols = rows - width
    marks = count // CHUNKS
    for j in range(count):
        g = j // marks
        if g == CHUNKS - 1:
            full = raw_ref[j]
        else:
            high, low = split(raw_ref[j, :width])
            full = compose_into(suffix_ref[g], high, low, raw_ref[j, width:], width)
        high, low = split(full[:width])
        zh_ref[j] = high
        zl_ref[j] = low
        zu_ref[j] = full[width:]
    steps = in_ref.shape[0]
    segs = steps // SEG

    def flip(s, _):
        block = jnp.concatenate([in_ref[m * SEG + s] for m in range(segs)], axis=0)
        flip_ref[s] = block.T
        return 0

    lax.fori_loop(0, SEG, flip, 0)


def compose_kernel(first_ref, second_ref, out_ref):
    width = first_ref.shape[1]
    high, low = split(second_ref[:width])
    rows = first_ref.shape[0]
    out = mm3(first_ref[...], high, low)
    if rows > width:
        out_ref[:width] = out[:width]
        out_ref[width:] = out[width:] + second_ref[width:]
    else:
        out_ref[...] = out + second_ref[width:]


def sweep_kernel(v_ref, zh_ref, zl_ref, zu_ref, rot_ref, d_ref, f_ref, flip_ref, adj_ref, grad_ref, cur):
    count, width = zh_ref.shape[0], zh_ref.shape[1]
    cols = v_ref.shape[0]
    v = v_ref[...]
    v_high, v_low = split(v)
    lows = []
    for j in range(count):
        z = mm(v_high, zh_ref[j]) + mm(v_low, zh_ref[j]) + mm(v_high, zl_ref[j]) + zu_ref[j]
        if j > 0:
            cur[(j - 1) * cols : j * cols] = z
        low = z.astype(BF16)
        adj_ref[j * SEG] = low
        lows.append(low)
    cur[(count - 1) * cols :] = v
    grad = mm(flip_ref[0], jnp.concatenate(lows, axis=0))
    for s in range(SEG - 1):
        at = SEG - 1 - s
        scaled = jnp.concatenate(
            [cur[m * cols : (m + 1) * cols] * d_ref[m * SEG + at : m * SEG + at + 1, :] for m in range(count)],
            axis=0,
        )
        out = mm3(scaled, rot_ref[0], rot_ref[1])
        force = jnp.concatenate([f_ref[m * SEG + at] for m in range(count)], axis=0)
        out = out + force.astype(F32)
        cur[...] = out
        low = out.astype(BF16)
        for m in range(count):
            adj_ref[m * SEG + at] = low[m * cols : (m + 1) * cols]
        grad = grad + mm(flip_ref[at], low)
    grad_ref[...] = grad.T


def vmem(n):
    return [pl.BlockSpec(memory_space=pltpu.VMEM)] * n


def params():
    return pltpu.CompilerParams(vmem_limit_bytes=VMEM_LIMIT)


def shape(dims, kind=F32):
    return jax.ShapeDtypeStruct(dims, kind)


def build(gen, derivs, force):
    steps, width = derivs.shape
    cols = force.shape[1]
    rows = width + cols
    return pl.pallas_call(
        build_kernel,
        out_shape=(
            shape((rows, width)),
            shape((steps // SEG, rows, width)),
            shape((CHUNKS - 1, rows, width)),
            shape((2, width, width), BF16),
        ),
        in_specs=vmem(3),
        out_specs=tuple(vmem(4)),
        scratch_shapes=[pltpu.VMEM((CHUNKS, rows, width), F32)],
        compiler_params=params(),
        name="build",
    )(gen, derivs, force)


def mark_maps(raw, suffix, ins):
    count, rows, width = raw.shape
    steps, cols, feats = ins.shape
    return pl.pallas_call(
        marks_kernel,
        out_shape=(
            shape((count, width, width), BF16),
            shape((count, width, width), BF16),
            shape((count, rows - width, width)),
            shape((SEG, feats, steps // SEG * cols), BF16),
        ),
        in_specs=vmem(3),
        out_specs=tuple(vmem(4)),
        compiler_params=params(),
        cost_estimate=pl.CostEstimate(flops=6 * count * rows * width * width, bytes_accessed=20_000_000, transcendentals=0),
        name="marks",
    )(raw, suffix, ins)


def compose(first, second):
    rows, width = first.shape
    return pl.pallas_call(
        compose_kernel,
        out_shape=shape((rows, width)),
        in_specs=vmem(2),
        out_specs=vmem(1)[0],
        compiler_params=params(),
        name="compose",
    )(first, second)


def sweep(v, zh, zl, zu, rot, derivs, force, flipped):
    steps, cols, width = force.shape
    feats = flipped.shape[1]
    return pl.pallas_call(
        sweep_kernel,
        out_shape=(shape((steps, cols, width), BF16), shape((width, feats))),
        in_specs=vmem(8),
        out_specs=tuple(vmem(2)),
        scratch_shapes=[pltpu.VMEM((steps // SEG * cols, width), F32)],
        compiler_params=params(),
        name="sweep",
    )(v, zh, zl, zu, rot, derivs, force, flipped)


def swap(x, bit):
    n = lax.axis_size("tm")
    return lax.ppermute(x, "tm", [(i, i ^ bit) for i in range(n)])


def incoming(own, terminal):
    n = lax.axis_size("tm")
    place = lax.axis_index("tm")
    rows, width = own.shape
    ident = jnp.concatenate(
        [jnp.eye(width, dtype=F32), jnp.zeros((rows - width, width), F32)], axis=0
    )
    total, later = own, ident
    bit = 1
    while bit < n // 2:
        other = swap(total, bit)
        early = (place & bit) == 0
        later = jnp.where(early, compose(other, later), later)
        total = compose(jnp.where(early, other, total), jnp.where(early, total, other))
        bit *= 2
    if n > 1:
        top = swap(compose(terminal, total), bit)
        terminal = jnp.where((place & bit) == 0, top, terminal)
    return compose(terminal, later)


def all_sum(x):
    n = lax.axis_size("tm")
    place = lax.axis_index("tm")
    halves = []
    bit = 1
    while bit < n and len(halves) < 2:
        half = x.shape[0] // 2
        upper = (place & bit) != 0
        keep = jnp.where(upper, x[half:], x[:half])
        give = jnp.where(upper, x[:half], x[half:])
        x = keep + swap(give, bit)
        halves.append((bit, upper))
        bit *= 2
    while bit < n:
        x = x + swap(x, bit)
        bit *= 2
    for at, upper in reversed(halves):
        other = swap(x, at)
        x = jnp.where(upper, jnp.concatenate([other, x], 0), jnp.concatenate([x, other], 0))
    return x


def body(generator, derivs, forcing, inputs, terminal):
    force = jnp.transpose(forcing, (0, 2, 1))
    ins = jnp.transpose(inputs, (0, 2, 1))
    own, raw, suffix, rot = build(generator, derivs, force)
    zh, zl, zu, flipped = mark_maps(raw, suffix, ins)
    v = incoming(own, terminal.T)
    adj, grad = sweep(v, zh, zl, zu, rot, derivs, force, flipped)
    return jnp.transpose(adj, (0, 2, 1)), all_sum(grad)


def solution(mesh):
    in_specs = (
        P(),
        P(("groups", "tm"), None),
        P(("groups", "tm"), None, None),
        P(("groups", "tm"), None, None),
        P("groups", None),
    )
    out_specs = (P(("groups", "tm"), None, None), P("groups", None))
    return jax.shard_map(body, mesh=mesh, in_specs=in_specs, out_specs=out_specs, check_vma=False)
```

```python
import functools
import math

import jax
import jax.numpy as jnp
from jax import lax
from jax.experimental import pallas as pl
from jax.experimental.pallas import tpu as pltpu
from jax.sharding import PartitionSpec as P

F32 = jnp.float32
BF16 = jnp.bfloat16
VMEM_LIMIT = 24 * 1024 * 1024
CHUNKS = 4
SEG = 8


def mm(a, b):
    return jnp.dot(a, b, preferred_element_type=F32)


def full_mm(a, b):
    return jnp.dot(a, b, precision=lax.Precision.HIGHEST, preferred_element_type=F32)


def split(x):
    high = x.astype(BF16)
    low = (x - high.astype(F32)).astype(BF16)
    return high, low


def mm3(a, b_high, b_low):
    a_high, a_low = split(a)
    return mm(a_high, b_high) + mm(a_low, b_high) + mm(a_high, b_low)


def rotation(gen):
    n = gen.shape[0]
    skew = gen - gen.T
    ident = (
        lax.broadcasted_iota(jnp.int32, (n, n), 0) == lax.broadcasted_iota(jnp.int32, (n, n), 1)
    ).astype(F32)
    c = [1.0 / math.factorial(k) for k in range(13)]
    s2 = full_mm(skew, skew)
    s3 = full_mm(s2, skew)
    s4 = full_mm(s2, s2)
    top = c[8] * ident + c[9] * skew + c[10] * s2 + c[11] * s3 + c[12] * s4
    mid = c[4] * ident + c[5] * skew + c[6] * s2 + c[7] * s3
    bottom = ident + skew + c[2] * s2 + c[3] * s3
    return bottom + full_mm(s4, mid + full_mm(s4, top)), ident


def compose(rows_in, through, width):
    high, low = split(through[:width])
    out = mm3(rows_in, high, low)
    return jnp.concatenate([out[:width], out[width:] + through[width:]], axis=0)


def apply(vec, through, width):
    high, low = split(through[:width])
    return mm3(vec, high, low) + through[width:]


def build_kernel(gen_ref, d_ref, f_hbm, map_ref, raw_ref, suffix_ref, rot_ref, f_ref, sem):
    steps, width = d_ref.shape
    per = steps // CHUNKS
    marks = per // SEG
    fetch = pltpu.make_async_copy(f_hbm, f_ref, sem)
    fetch.start()
    rot, ident = rotation(gen_ref[...])
    rot_high, rot_low = split(rot)
    rot_ref[0] = rot_high
    rot_ref[1] = rot_low
    fetch.wait()

    def run(k, states):
        for s in range(SEG):
            out = []
            for g in range(CHUNKS):
                t = g * per + per - 1 - k * SEG - s
                moved = mm3(states[g] * d_ref[pl.ds(t, 1), :], rot_ref[0], rot_ref[1])
                out.append(
                    jnp.concatenate([moved[:width], moved[width:] + f_ref[t].astype(F32)], axis=0)
                )
            states = out
        for g in range(CHUNKS):
            raw_ref[g * marks + marks - 1 - k] = states[g]

    first = jnp.concatenate([ident, jnp.zeros((f_ref.shape[1], width), F32)], axis=0)
    run(0, [first] * CHUNKS)

    def more(k, _):
        run(k, [raw_ref[g * marks + marks - k] for g in range(CHUNKS)])
        return 0

    lax.fori_loop(1, marks, more, 0)
    acc = raw_ref[(CHUNKS - 1) * marks]
    for g in range(CHUNKS - 2, -1, -1):
        suffix_ref[g] = acc
        acc = compose(acc, raw_ref[g * marks], width)
    map_ref[...] = acc


def marks_kernel(raw_ref, suffix_ref, in_hbm, zh_ref, zl_ref, zu_ref, flip_ref, in_ref, sem):
    fetch = pltpu.make_async_copy(in_hbm, in_ref, sem)
    fetch.start()
    count, rows, width = raw_ref.shape
    marks = count // CHUNKS
    for j in range(count):
        g = j // marks
        full = raw_ref[j]
        if g < CHUNKS - 1:
            full = compose(suffix_ref[g], full, width)
        high, low = split(full[:width])
        zh_ref[j] = high
        zl_ref[j] = low
        zu_ref[j] = full[width:]
    fetch.wait()
    segs = in_ref.shape[0] // SEG
    for s in range(SEG):
        block = jnp.concatenate([in_ref[m * SEG + s] for m in range(segs)], axis=0)
        flip_ref[s] = block.T


def early(bit):
    return (lax.axis_index("tm") & bit) == 0


def merge_kernel(bit, own_ref, other_ref, out_ref):
    width = own_ref.shape[1]
    first = early(bit)

    @pl.when(first)
    def _():
        out_ref[...] = compose(other_ref[...], own_ref[...], width)

    @pl.when(jnp.logical_not(first))
    def _():
        out_ref[...] = compose(own_ref[...], other_ref[...], width)


def top_kernel(bit, vec_ref, own_ref, other_ref, out_ref):
    width = own_ref.shape[1]
    first = early(bit)

    @pl.when(first)
    def _():
        out_ref[...] = apply(apply(vec_ref[...], other_ref[...], width), own_ref[...], width)

    @pl.when(jnp.logical_not(first))
    def _():
        out_ref[...] = apply(apply(vec_ref[...], own_ref[...], width), other_ref[...], width)


def later_kernel(bit, other_ref, later_ref, out_ref):
    width = other_ref.shape[1]
    first = early(bit)

    @pl.when(first)
    def _():
        out_ref[...] = compose(other_ref[...], later_ref[...], width)

    @pl.when(jnp.logical_not(first))
    def _():
        out_ref[...] = later_ref[...]


def first_later_kernel(bit, other_ref, out_ref):
    rows, width = other_ref.shape
    first = early(bit)

    @pl.when(first)
    def _():
        out_ref[...] = other_ref[...]

    @pl.when(jnp.logical_not(first))
    def _():
        out_ref[...] = (
            lax.broadcasted_iota(jnp.int32, (rows, width), 0) == lax.broadcasted_iota(jnp.int32, (rows, width), 1)
        ).astype(F32)


def sweep_kernel(
    bit, end_ref, got_ref, later_ref, zh_ref, zl_ref, zu_ref, rot_ref, d_ref, f_ref, flip_ref,
    adj_hbm, keep_ref, give_ref, cur, low_ref, sems,
):
    count, width = zh_ref.shape[0], zh_ref.shape[1]
    cols = end_ref.shape[0]
    v = jnp.where(early(bit), got_ref[...], end_ref[...])
    v = apply(v, later_ref[...], width)
    v_high, v_low = split(v)

    def send(at):
        return pltpu.make_async_copy(low_ref.at[at], adj_hbm.at[:, at], sems.at[at])

    for j in range(count):
        z = mm(v_high, zh_ref[j]) + mm(v_low, zh_ref[j]) + mm(v_high, zl_ref[j]) + zu_ref[j]
        if j > 0:
            cur[j - 1] = z
        low_ref[0, j] = z.astype(BF16)
    cur[count - 1] = v
    send(0).start()
    grad = mm(flip_ref[0], low_ref[0].reshape(count * cols, width))
    pack = 4
    for s in range(SEG - 1):
        at = SEG - 1 - s
        for p in range(0, count, pack):
            scaled = jnp.concatenate(
                [cur[m] * d_ref[m * SEG + at : m * SEG + at + 1, :] for m in range(p, p + pack)], axis=0
            )
            out = mm3(scaled, rot_ref[0], rot_ref[1])
            for m in range(p, p + pack):
                value = out[(m - p) * cols : (m - p + 1) * cols] + f_ref[m * SEG + at].astype(F32)
                cur[m] = value
                low_ref[at, m] = value.astype(BF16)
        send(at).start()
        grad = grad + mm(flip_ref[at], low_ref[at].reshape(count * cols, width))
    grad = grad.T
    half = width // 2
    first = early(1)
    keep_ref[...] = jnp.where(first, grad[:half], grad[half:])
    give_ref[...] = jnp.where(first, grad[half:], grad[:half])
    for at in range(SEG):
        send(at).wait()


def halve_kernel(bit, keep_ref, got_ref, mine_ref, give_ref):
    total = keep_ref[...] + got_ref[...]
    half = total.shape[0] // 2
    first = early(bit)
    mine_ref[...] = jnp.where(first, total[:half], total[half:])
    give_ref[...] = jnp.where(first, total[half:], total[:half])


def join_kernel(own_ref, far_ref, core_ref, both_ref, out_ref):
    rows = own_ref.shape[0]
    place = lax.axis_index("tm")
    low, high = place & 1, (place // 2) & 1
    for ref, a, b in (
        (own_ref, low, high),
        (far_ref, low, 1 - high),
        (core_ref, 1 - low, high),
        (both_ref, 1 - low, 1 - high),
    ):
        out_ref[pl.ds(pl.multiple_of((2 * a + b) * rows, rows), rows), :] = ref[...]


VM = pltpu.VMEM


def near(x):
    return pltpu.with_memory_space_constraint(x, VM)


def call(kernel, name, out, *args, where=None, scratch=(), flops=0, data=0):
    where = where or {}
    ins = [pl.BlockSpec(memory_space=pl.ANY if i in where else VM) for i in range(len(args))]
    args = [a if i in where else near(a) for i, a in enumerate(args)]
    outs = tuple(
        pl.BlockSpec(memory_space=pl.ANY if isinstance(o, jax.ShapeDtypeStruct) and len(o.shape) > 2 else VM)
        for o in out
    )
    return pl.pallas_call(
        kernel,
        out_shape=tuple(out),
        in_specs=ins,
        out_specs=outs,
        scratch_shapes=list(scratch),
        compiler_params=pltpu.CompilerParams(vmem_limit_bytes=VMEM_LIMIT),
        cost_estimate=pl.CostEstimate(flops=flops, bytes_accessed=data, transcendentals=0),
        name=name,
    )(*args)


def build(gen, derivs, force):
    steps, width = derivs.shape
    cols = force.shape[1]
    rows = width + cols
    return call(
        build_kernel,
        "build",
        (
            VM((rows, width), F32),
            VM((steps // SEG, rows, width), F32),
            VM((CHUNKS - 1, rows, width), F32),
            VM((2, width, width), BF16),
            VM(force.shape, BF16),
        ),
        gen,
        derivs,
        force,
        where={2},
        scratch=[pltpu.SemaphoreType.DMA],
        flops=6 * steps * rows * width * width,
    )


def mark_maps(raw, suffix, ins):
    count, rows, width = raw.shape
    steps, cols, feats = ins.shape
    return call(
        marks_kernel,
        "marks",
        (
            VM((count, width, width), BF16),
            VM((count, width, width), BF16),
            VM((count, rows - width, width), F32),
            VM((SEG, feats, steps // SEG * cols), BF16),
        ),
        raw,
        suffix,
        ins,
        where={2},
        scratch=[VM(ins.shape, BF16), pltpu.SemaphoreType.DMA],
        flops=6 * count * rows * width * width,
        data=15_000_000,
    )


def sweep(bit, end, got, later, zh, zl, zu, rot, derivs, force, flipped):
    steps, cols, width = force.shape
    feats = flipped.shape[1]
    segs = steps // SEG
    adj, keep, give = call(
        functools.partial(sweep_kernel, bit),
        "sweep",
        (
            shape((segs, SEG, cols, width), BF16),
            VM((width // 2, feats), F32),
            VM((width // 2, feats), F32),
        ),
        end, got, later, zh, zl, zu, rot, derivs, force, flipped,
        scratch=[
            VM((segs, cols, width), F32),
            VM((SEG, segs, cols, width), BF16),
            pltpu.SemaphoreType.DMA((SEG,)),
        ],
        flops=8 * steps * cols * width * width,
    )
    return adj.reshape(steps, cols, width), keep, give


def shape(dims, kind=F32):
    return jax.ShapeDtypeStruct(dims, kind)


def swap(x, bit):
    n = lax.axis_size("tm")
    return lax.ppermute(x, "tm", [(i, i ^ bit) for i in range(n)])


def incoming(own, terminal):
    n = lax.axis_size("tm")
    rows, width = own.shape
    flops = 6 * rows * width * width
    bits = [1 << k for k in range(n.bit_length() - 1)]
    total, later, top = own, None, None
    vec = VM(terminal.shape, F32)
    whole = VM(own.shape, F32)
    for bit in bits[:-1]:
        other = swap(total, bit)
        if later is None:
            (later,) = call(functools.partial(first_later_kernel, bit), "later", (whole,), other)
        else:
            (later,) = call(functools.partial(later_kernel, bit), "later", (whole,), other, later, flops=flops)
        if bit < bits[-2]:
            (total,) = call(functools.partial(merge_kernel, bit), "merge", (whole,), total, other, flops=flops)
        else:
            (top,) = call(functools.partial(top_kernel, bit), "top", (vec,), terminal, total, other, flops=flops // 5)
    return bits[-1], swap(top, bits[-1]), later


def all_sum(keep, give):
    n = lax.axis_size("tm")
    quarter = VM((keep.shape[0] // 2, keep.shape[1]), F32)
    mine, give = call(functools.partial(halve_kernel, 2), "halve", (quarter, quarter), keep, swap(give, 1))
    x = mine + swap(give, 2)
    bit = 4
    while bit < n:
        x = x + swap(x, bit)
        bit *= 2
    far = swap(x, 2)
    core = swap(x, 1)
    both = swap(far, 1)
    (out,) = call(join_kernel, "join", (shape((4 * x.shape[0], x.shape[1])),), x, far, core, both)
    return out


def body(generator, derivs, forcing, inputs, terminal):
    force = jnp.transpose(forcing, (0, 2, 1))
    ins = jnp.transpose(inputs, (0, 2, 1))
    end = terminal.T
    own, raw, suffix, rot, force = build(generator, derivs, force)
    zh, zl, zu, flipped = mark_maps(raw, suffix, ins)
    bit, got, later = incoming(own, end)
    adj, keep, give = sweep(bit, end, got, later, zh, zl, zu, rot, derivs, force, flipped)
    return jnp.transpose(adj, (0, 2, 1)), all_sum(keep, give)


def solution(mesh):
    in_specs = (
        P(),
        P(("groups", "tm"), None),
        P(("groups", "tm"), None, None),
        P(("groups", "tm"), None, None),
        P("groups", None),
    )
    out_specs = (P(("groups", "tm"), None, None), P("groups", None))
    return jax.shard_map(body, mesh=mesh, in_specs=in_specs, out_specs=out_specs, check_vma=False)
```

```python
import functools
import math

import jax
import jax.numpy as jnp
from jax import lax
from jax.experimental import pallas as pl
from jax.experimental.pallas import tpu as pltpu
from jax.sharding import PartitionSpec as P

F32 = jnp.float32
BF16 = jnp.bfloat16
VMEM_LIMIT = 24 * 1024 * 1024
CHUNKS = 4
SEG = 8


def mm(a, b):
    return jnp.dot(a, b, preferred_element_type=F32)


def split(x):
    high = x.astype(BF16)
    low = (x - high.astype(F32)).astype(BF16)
    return high, low


def mm3(a, b_high, b_low):
    a_high, a_low = split(a)
    return mm(a_high, b_high) + mm(a_low, b_high) + mm(a_high, b_low)


def rotation(gen):
    n = gen.shape[0]
    skew = gen - gen.T
    ident = (
        lax.broadcasted_iota(jnp.int32, (n, n), 0) == lax.broadcasted_iota(jnp.int32, (n, n), 1)
    ).astype(F32)
    c = [1.0 / math.factorial(k) for k in range(13)]
    halves = split(skew)
    s2 = mm3(skew, *halves)
    s3 = mm3(s2, *halves)
    s4 = mm3(s2, *split(s2))
    top = c[8] * ident + c[9] * skew + c[10] * s2 + c[11] * s3 + c[12] * s4
    mid = c[4] * ident + c[5] * skew + c[6] * s2 + c[7] * s3
    bottom = ident + skew + c[2] * s2 + c[3] * s3
    inner = mid + mm3(s4, *split(top))
    return bottom + mm3(s4, *split(inner))


def compose(rows_in, through, width):
    high, low = split(through[:width])
    out = mm3(rows_in, high, low)
    return jnp.concatenate([out[:width], out[width:] + through[width:]], axis=0)


def apply(vec, through, width):
    high, low = split(through[:width])
    return mm3(vec, high, low) + through[width:]


def build_kernel(gen_hbm, d_hbm, f_hbm, map_ref, raw_ref, suffix_ref, rot_ref, d_ref, f_ref, gen_ref, sems):
    steps, width = d_ref.shape
    per = steps // CHUNKS
    marks = per // SEG
    fetches = [
        pltpu.make_async_copy(far, here, sems.at[i])
        for i, (far, here) in enumerate(((gen_hbm, gen_ref), (d_hbm, d_ref), (f_hbm, f_ref)))
    ]
    for fetch in fetches:
        fetch.start()
    fetches[0].wait()
    rot = rotation(gen_ref[...])
    rot_high, rot_low = split(rot)
    rot_ref[0] = rot_high
    rot_ref[1] = rot_low
    fetches[1].wait()
    fetches[2].wait()

    def run(k, states, done):
        for s in range(done, SEG):
            out = []
            for g in range(CHUNKS):
                t = g * per + per - 1 - k * SEG - s
                moved = mm3(states[g] * d_ref[pl.ds(t, 1), :], rot_ref[0], rot_ref[1])
                out.append(
                    jnp.concatenate([moved[:width], moved[width:] + f_ref[t].astype(F32)], axis=0)
                )
            states = out
        for g in range(CHUNKS):
            raw_ref[g * marks + marks - 1 - k] = states[g]

    first = []
    for g in range(CHUNKS):
        end = (g + 1) * per
        column = d_ref[end - 8 : end, :].T[:, 7:8]
        first.append(jnp.concatenate([rot * column, f_ref[end - 1].astype(F32)], axis=0))
    run(0, first, 1)

    def more(k, _):
        run(k, [raw_ref[g * marks + marks - k] for g in range(CHUNKS)], 0)
        return 0

    lax.fori_loop(1, marks, more, 0)
    acc = raw_ref[(CHUNKS - 1) * marks]
    for g in range(CHUNKS - 2, -1, -1):
        suffix_ref[g] = acc
        acc = compose(acc, raw_ref[g * marks], width)
    map_ref[...] = acc


def marks_kernel(raw_ref, suffix_ref, in_hbm, zh_ref, zl_ref, zu_ref, flip_ref, in_ref, sem):
    fetch = pltpu.make_async_copy(in_hbm, in_ref, sem)
    fetch.start()
    count, rows, width = raw_ref.shape
    marks = count // CHUNKS
    for j in range(count):
        g = j // marks
        full = raw_ref[j]
        if g < CHUNKS - 1:
            full = compose(suffix_ref[g], full, width)
        high, low = split(full[:width])
        zh_ref[j] = high
        zl_ref[j] = low
        zu_ref[j] = full[width:]
    fetch.wait()
    segs = in_ref.shape[0] // SEG
    for s in range(SEG):
        block = jnp.concatenate([in_ref[m * SEG + s] for m in range(segs)], axis=0)
        flip_ref[s] = block.T


def early(bit):
    return (lax.axis_index("tm") & bit) == 0


def merge_kernel(bit, own_ref, other_ref, out_ref):
    width = own_ref.shape[1]
    first = early(bit)

    @pl.when(first)
    def _():
        out_ref[...] = compose(other_ref[...], own_ref[...], width)

    @pl.when(jnp.logical_not(first))
    def _():
        out_ref[...] = compose(own_ref[...], other_ref[...], width)


def end_kernel(bit, own_ref, other_ref, vec_ref, out_ref, through_ref):
    merge_kernel(bit, own_ref, other_ref, out_ref)
    through_ref[...] = apply(vec_ref[...], out_ref[...], own_ref.shape[1])


def apply_kernel(vec_ref, map_ref, out_ref):
    out_ref[...] = apply(vec_ref[...], map_ref[...], map_ref.shape[1])


def later_kernel(quarter, other_ref, later_ref, out_ref):
    bit, only = quarter
    width = other_ref.shape[1]
    first = lax.axis_index("tm") < only if only else early(bit)

    @pl.when(first)
    def _():
        out_ref[...] = compose(other_ref[...], later_ref[...], width)

    @pl.when(jnp.logical_not(first))
    def _():
        out_ref[...] = later_ref[...]


def first_later_kernel(bit, other_ref, out_ref):
    rows, width = other_ref.shape
    first = early(bit)

    @pl.when(first)
    def _():
        out_ref[...] = other_ref[...]

    @pl.when(jnp.logical_not(first))
    def _():
        out_ref[...] = (
            lax.broadcasted_iota(jnp.int32, (rows, width), 0) == lax.broadcasted_iota(jnp.int32, (rows, width), 1)
        ).astype(F32)


def sweep_kernel(
    part, end_ref, got_ref, up_ref, down_ref, later_ref, zh_ref, zl_ref, zu_ref,
    rot_ref, d_ref, f_ref, flip_ref,
    adj_hbm, keep_ref, give_ref, cur, low_ref, sems,
):
    count, width = zh_ref.shape[0], zh_ref.shape[1]
    cols = end_ref.shape[0]
    place = lax.axis_index("tm") // part
    v = jnp.where(place == 3, end_ref[...], got_ref[...])
    v = jnp.where(place == 1, up_ref[...], v)
    v = jnp.where(place == 0, down_ref[...], v)
    v = apply(v, later_ref[...], width)
    v_high, v_low = split(v)

    def send(at):
        return pltpu.make_async_copy(low_ref.at[at], adj_hbm.at[:, at], sems.at[at])

    for j in range(count):
        z = mm(v_high, zh_ref[j]) + mm(v_low, zh_ref[j]) + mm(v_high, zl_ref[j]) + zu_ref[j]
        if j > 0:
            cur[j - 1] = z
        low_ref[0, j] = z.astype(BF16)
    cur[count - 1] = v
    send(0).start()
    grad = mm(flip_ref[0], low_ref[0].reshape(count * cols, width))
    pack = 4
    for s in range(SEG - 1):
        at = SEG - 1 - s
        for p in range(0, count, pack):
            scaled = jnp.concatenate(
                [cur[m] * d_ref[m * SEG + at : m * SEG + at + 1, :] for m in range(p, p + pack)], axis=0
            )
            out = mm3(scaled, rot_ref[0], rot_ref[1])
            for m in range(p, p + pack):
                value = out[(m - p) * cols : (m - p + 1) * cols] + f_ref[m * SEG + at].astype(F32)
                cur[m] = value
                low_ref[at, m] = value.astype(BF16)
        send(at).start()
        grad = grad + mm(flip_ref[at], low_ref[at].reshape(count * cols, width))
    grad = grad.T
    half = width // 2
    first = early(1)
    keep_ref[...] = jnp.where(first, grad[:half], grad[half:])
    give_ref[...] = jnp.where(first, grad[half:], grad[:half])
    for at in range(SEG):
        send(at).wait()


def halve_kernel(bit, keep_ref, got_ref, mine_ref, give_ref):
    total = keep_ref[...] + got_ref[...]
    half = total.shape[0] // 2
    first = early(bit)
    mine_ref[...] = jnp.where(first, total[:half], total[half:])
    give_ref[...] = jnp.where(first, total[half:], total[:half])


def join_kernel(own_ref, far_ref, core_ref, both_ref, out_ref):
    rows = own_ref.shape[0]
    place = lax.axis_index("tm")
    low, high = place & 1, (place // 2) & 1
    for ref, a, b in (
        (own_ref, low, high),
        (far_ref, low, 1 - high),
        (core_ref, 1 - low, high),
        (both_ref, 1 - low, 1 - high),
    ):
        out_ref[pl.ds(pl.multiple_of((2 * a + b) * rows, rows), rows), :] = ref[...]


VM = pltpu.VMEM


def call(kernel, name, out, *args, where=None, scratch=(), flops=0, data=0):
    where = where or {}
    ins = [pl.BlockSpec(memory_space=pl.ANY if i in where else VM) for i in range(len(args))]
    args = [pltpu.with_memory_space_constraint(a, pltpu.HBM if i in where else VM) for i, a in enumerate(args)]
    outs = tuple(
        pl.BlockSpec(memory_space=pl.ANY if isinstance(o, jax.ShapeDtypeStruct) and len(o.shape) > 2 else VM)
        for o in out
    )
    return pl.pallas_call(
        kernel,
        out_shape=tuple(out),
        in_specs=ins,
        out_specs=outs,
        scratch_shapes=list(scratch),
        compiler_params=pltpu.CompilerParams(vmem_limit_bytes=VMEM_LIMIT),
        cost_estimate=pl.CostEstimate(flops=flops, bytes_accessed=data, transcendentals=0),
        name=name,
    )(*args)


def build(gen, derivs, force):
    steps, width = derivs.shape
    cols = force.shape[1]
    rows = width + cols
    return call(
        build_kernel,
        "build",
        (
            VM((rows, width), F32),
            VM((steps // SEG, rows, width), F32),
            VM((CHUNKS - 1, rows, width), F32),
            VM((2, width, width), BF16),
            VM(derivs.shape, F32),
            VM(force.shape, BF16),
        ),
        gen,
        derivs,
        force,
        where={0, 1, 2},
        scratch=[VM(gen.shape, F32), pltpu.SemaphoreType.DMA((3,))],
        flops=6 * steps * rows * width * width,
    )


def mark_maps(raw, suffix, ins):
    count, rows, width = raw.shape
    steps, cols, feats = ins.shape
    return call(
        marks_kernel,
        "marks",
        (
            VM((count, width, width), BF16),
            VM((count, width, width), BF16),
            VM((count, rows - width, width), F32),
            VM((SEG, feats, steps // SEG * cols), BF16),
        ),
        raw,
        suffix,
        ins,
        where={2},
        scratch=[VM(ins.shape, BF16), pltpu.SemaphoreType.DMA],
        flops=6 * count * rows * width * width,
        data=15_000_000,
    )


def sweep(entering, later, zh, zl, zu, rot, derivs, force, flipped):
    steps, cols, width = force.shape
    feats = flipped.shape[1]
    segs = steps // SEG
    adj, keep, give = call(
        functools.partial(sweep_kernel, lax.axis_size("tm") // 4),
        "sweep",
        (
            shape((segs, SEG, cols, width), BF16),
            VM((width // 2, feats), F32),
            VM((width // 2, feats), F32),
        ),
        *entering, later, zh, zl, zu, rot, derivs, force, flipped,
        scratch=[
            VM((segs, cols, width), F32),
            VM((SEG, segs, cols, width), BF16),
            pltpu.SemaphoreType.DMA((SEG,)),
        ],
        flops=8 * steps * cols * width * width,
    )
    return adj.reshape(steps, cols, width), keep, give


def shape(dims, kind=F32):
    return jax.ShapeDtypeStruct(dims, kind)


def swap(x, bit):
    n = lax.axis_size("tm")
    return lax.ppermute(x, "tm", [(i, i ^ bit) for i in range(n)])


def incoming(own, end):
    n = lax.axis_size("tm")
    part = n // 4
    rows, width = own.shape
    flops = 6 * rows * width * width
    vec = VM(end.shape, F32)
    whole = VM(own.shape, F32)
    total, later, bit = own, None, 1
    while bit < part:
        other = swap(total, bit)
        if later is None:
            (later,) = call(functools.partial(first_later_kernel, bit), "later", (whole,), other)
        else:
            (later,) = call(functools.partial(later_kernel, (bit, 0)), "later", (whole,), other, later, flops=flops)
        if 2 * bit < part:
            (total,) = call(functools.partial(merge_kernel, bit), "merge", (whole,), total, other, flops=flops)
        else:
            total, last = call(
                functools.partial(end_kernel, bit), "end", (whole, vec), total, other, end, flops=flops
            )
        bit *= 2
    got = lax.ppermute(last, "tm", [(i + 3 * part, i + 2 * part) for i in range(part)])
    second = lax.ppermute(total, "tm", [(i + part, i) for i in range(part)])
    (top,) = call(apply_kernel, "top", (vec,), got, total, flops=flops // 5)
    up = lax.ppermute(top, "tm", [(i + 2 * part, i + part) for i in range(part)])
    down = lax.ppermute(top, "tm", [(i + 2 * part, i) for i in range(part)])
    (later,) = call(functools.partial(later_kernel, (0, part)), "later", (whole,), second, later, flops=flops)
    return (end, got, up, down), later


def all_sum(keep, give):
    n = lax.axis_size("tm")
    quarter = VM((keep.shape[0] // 2, keep.shape[1]), F32)
    mine, give = call(functools.partial(halve_kernel, 2), "halve", (quarter, quarter), keep, swap(give, 1))
    x = mine + swap(give, 2)
    bit = 4
    while bit < n:
        x = x + swap(x, bit)
        bit *= 2
    far = swap(x, 2)
    core = swap(x, 1)
    both = swap(far, 1)
    (out,) = call(join_kernel, "join", (shape((4 * x.shape[0], x.shape[1])),), x, far, core, both)
    return out


def body(generator, derivs, forcing, inputs, terminal):
    force = jnp.transpose(forcing, (0, 2, 1))
    ins = jnp.transpose(inputs, (0, 2, 1))
    end = terminal.T
    own, raw, suffix, rot, derivs, force = build(generator, derivs, force)
    zh, zl, zu, flipped = mark_maps(raw, suffix, ins)
    entering, later = incoming(own, end)
    adj, keep, give = sweep(entering, later, zh, zl, zu, rot, derivs, force, flipped)
    return jnp.transpose(adj, (0, 2, 1)), all_sum(keep, give)


def solution(mesh):
    in_specs = (
        P(),
        P(("groups", "tm"), None),
        P(("groups", "tm"), None, None),
        P(("groups", "tm"), None, None),
        P("groups", None),
    )
    out_specs = (P(("groups", "tm"), None, None), P("groups", None))
    return jax.shard_map(body, mesh=mesh, in_specs=in_specs, out_specs=out_specs, check_vma=False)
```

```python
import functools
import math

import jax
import jax.numpy as jnp
from jax import lax
from jax.experimental import pallas as pl
from jax.experimental.pallas import tpu as pltpu
from jax.sharding import PartitionSpec as P

F32 = jnp.float32
BF16 = jnp.bfloat16
VMEM_LIMIT = 24 * 1024 * 1024
CHUNKS = 4
SEG = 8


def mm(a, b):
    return jnp.dot(a, b, preferred_element_type=F32)


def split(x):
    high = x.astype(BF16)
    low = (x - high.astype(F32)).astype(BF16)
    return high, low


def mm3(a, b_high, b_low):
    a_high, a_low = split(a)
    return mm(a_high, b_high) + mm(a_low, b_high) + mm(a_high, b_low)


def rotation(gen):
    n = gen.shape[0]
    skew = gen - gen.T
    ident = (
        lax.broadcasted_iota(jnp.int32, (n, n), 0) == lax.broadcasted_iota(jnp.int32, (n, n), 1)
    ).astype(F32)
    c = [1.0 / math.factorial(k) for k in range(13)]
    halves = split(skew)
    s2 = mm3(skew, *halves)
    s3 = mm3(s2, *halves)
    s4 = mm3(s2, *split(s2))
    top = c[8] * ident + c[9] * skew + c[10] * s2 + c[11] * s3 + c[12] * s4
    mid = c[4] * ident + c[5] * skew + c[6] * s2 + c[7] * s3
    bottom = ident + skew + c[2] * s2 + c[3] * s3
    inner = mid + mm3(s4, *split(top))
    return bottom + mm3(s4, *split(inner))


def compose(rows_in, through, width):
    high, low = split(through[:width])
    out = mm3(rows_in, high, low)
    return jnp.concatenate([out[:width], out[width:] + through[width:]], axis=0)


def apply(vec, through, width):
    high, low = split(through[:width])
    return mm3(vec, high, low) + through[width:]


def build_kernel(gen_hbm, d_hbm, f_hbm, map_ref, raw_ref, suffix_ref, rot_ref, d_ref, f_ref, gen_ref, sems):
    steps, width = d_ref.shape
    per = steps // CHUNKS
    marks = per // SEG
    fetches = [
        pltpu.make_async_copy(far, here, sems.at[i])
        for i, (far, here) in enumerate(((gen_hbm, gen_ref), (d_hbm, d_ref), (f_hbm, f_ref)))
    ]
    for fetch in fetches:
        fetch.start()
    fetches[0].wait()
    rot = rotation(gen_ref[...])
    rot_high, rot_low = split(rot)
    rot_ref[0] = rot_high
    rot_ref[1] = rot_low
    fetches[1].wait()
    fetches[2].wait()

    def run(k, states, done):
        for s in range(done, SEG):
            out = []
            for g in range(CHUNKS):
                t = g * per + per - 1 - k * SEG - s
                moved = mm3(states[g] * d_ref[pl.ds(t, 1), :], rot_ref[0], rot_ref[1])
                out.append(
                    jnp.concatenate([moved[:width], moved[width:] + f_ref[t].astype(F32)], axis=0)
                )
            states = out
        for g in range(CHUNKS):
            raw_ref[g * marks + marks - 1 - k] = states[g]

    first = []
    for g in range(CHUNKS):
        end = (g + 1) * per
        column = d_ref[end - 8 : end, :].T[:, 7:8]
        first.append(jnp.concatenate([rot * column, f_ref[end - 1].astype(F32)], axis=0))
    run(0, first, 1)

    def more(k, _):
        run(k, [raw_ref[g * marks + marks - k] for g in range(CHUNKS)], 0)
        return 0

    lax.fori_loop(1, marks, more, 0)
    acc = raw_ref[(CHUNKS - 1) * marks]
    for g in range(CHUNKS - 2, -1, -1):
        suffix_ref[g] = acc
        acc = compose(acc, raw_ref[g * marks], width)
    map_ref[...] = acc


def marks_kernel(raw_ref, suffix_ref, in_hbm, _, zh_ref, zl_ref, zu_ref, flip_ref, __, in_ref, sem):
    fetch = pltpu.make_async_copy(in_hbm, in_ref, sem)
    fetch.start()
    count, rows, width = raw_ref.shape
    marks = count // CHUNKS
    for j in range(count):
        g = j // marks
        full = raw_ref[j]
        if g < CHUNKS - 1:
            full = compose(suffix_ref[g], full, width)
        high, low = split(full[:width])
        zh_ref[j] = high
        zl_ref[j] = low
        zu_ref[j] = full[width:]
    fetch.wait()
    segs = in_ref.shape[0] // SEG
    for s in range(SEG):
        block = jnp.concatenate([in_ref[m * SEG + s] for m in range(segs)], axis=0)
        flip_ref[s] = block.T


def early(bit):
    return (lax.axis_index("tm") & bit) == 0


def core_half(x):
    half = x.shape[0] // 2
    return jnp.where(early(1), x[:half], x[half:])


def place_halves(mine, other, out_ref):
    half = mine.shape[0]
    start = pl.multiple_of((lax.axis_index("tm") & 1) * half, half)
    out_ref[pl.ds(start, half), :] = mine
    out_ref[pl.ds(pl.multiple_of(half - start, half), half), :] = other


def ordered(bit, own_ref, other_ref, out_ref):
    width = own_ref.shape[1]
    first = early(bit)

    @pl.when(first)
    def _():
        out_ref[...] = compose(other_ref[...], own_ref[...], width)

    @pl.when(jnp.logical_not(first))
    def _():
        out_ref[...] = compose(own_ref[...], other_ref[...], width)


def pair_kernel(own_ref, other_ref, out_ref, half_ref):
    ordered(1, own_ref, other_ref, out_ref)
    half_ref[...] = core_half(out_ref[...])


def position(low_bit, count):
    return (lax.axis_index("tm") // low_bit) % count


def group_maps(own_ref, halves, maps):
    maps[0] = own_ref[...]
    for mask in range(1, maps.shape[0]):
        place_halves(halves[2 * mask - 2][...], halves[2 * mask - 1][...], maps.at[mask])


def top_kernel(low_bit, own_ref, vec_ref, *rest):
    halves, (out_ref, maps) = rest[:-2], rest[-2:]
    group_maps(own_ref, halves, maps)
    count, _, width = maps.shape
    here = position(low_bit, count)
    vec = vec_ref[...]
    for at in range(count - 1, -1, -1):
        vec = apply(vec, maps[at ^ here], width)
    out_ref[...] = vec


def total_kernel(low_bit, own_ref, *rest):
    halves, (out_ref, half_ref, maps) = rest[:-3], rest[-3:]
    group_maps(own_ref, halves, maps)
    count, _, width = maps.shape
    here = position(low_bit, count)
    acc = maps[(count - 1) ^ here]
    for at in range(count - 2, -1, -1):
        acc = compose(acc, maps[at ^ here], width)
    out_ref[...] = acc
    half_ref[...] = core_half(acc)


def later_kernel(low_bit, later_ref, *rest):
    halves, (out_ref, maps) = rest[:-2], rest[-2:]
    count, _, width = maps.shape
    for mask in range(1, count):
        place_halves(halves[2 * mask - 2][...], halves[2 * mask - 1][...], maps.at[mask])
    here = position(low_bit, count)
    maps[0] = later_ref[...]
    out_ref[...] = maps[jnp.where(here == count - 1, 0, (count - 1) ^ here)]
    for at in range(count - 2, -1, -1):

        @pl.when(at >= here)
        def _():
            out_ref[...] = compose(out_ref[...], maps[at ^ here], width)


def first_later_kernel(bit, other_ref, out_ref):
    rows, width = other_ref.shape
    first = early(bit)

    @pl.when(first)
    def _():
        out_ref[...] = other_ref[...]

    @pl.when(jnp.logical_not(first))
    def _():
        out_ref[...] = (
            lax.broadcasted_iota(jnp.int32, (rows, width), 0) == lax.broadcasted_iota(jnp.int32, (rows, width), 1)
        ).astype(F32)


def sweep_kernel(
    bit, end_ref, got_ref, later_ref, zh_ref, zl_ref, zu_ref,
    rot_ref, d_ref, f_ref, flip_ref,
    adj_hbm, keep_ref, give_ref, cur, low_ref, sems,
):
    count, width = zh_ref.shape[0], zh_ref.shape[1]
    cols = end_ref.shape[0]
    v = jnp.where(early(bit), got_ref[...], end_ref[...])
    v = apply(v, later_ref[...], width)
    v_high, v_low = split(v)

    def send(at):
        return pltpu.make_async_copy(low_ref.at[at], adj_hbm.at[:, at], sems.at[at])

    for j in range(count):
        z = mm(v_high, zh_ref[j]) + mm(v_low, zh_ref[j]) + mm(v_high, zl_ref[j]) + zu_ref[j]
        if j > 0:
            cur[j - 1] = z
        low_ref[0, j] = z.astype(BF16)
    cur[count - 1] = v
    send(0).start()
    grad = mm(flip_ref[0], low_ref[0].reshape(count * cols, width))
    pack = 4
    for s in range(SEG - 1):
        at = SEG - 1 - s
        for p in range(0, count, pack):
            scaled = jnp.concatenate(
                [cur[m] * d_ref[m * SEG + at : m * SEG + at + 1, :] for m in range(p, p + pack)], axis=0
            )
            out = mm3(scaled, rot_ref[0], rot_ref[1])
            for m in range(p, p + pack):
                value = out[(m - p) * cols : (m - p + 1) * cols] + f_ref[m * SEG + at].astype(F32)
                cur[m] = value
                low_ref[at, m] = value.astype(BF16)
        send(at).start()
        grad = grad + mm(flip_ref[at], low_ref[at].reshape(count * cols, width))
    grad = grad.T
    half = width // 2
    first = early(1)
    keep_ref[...] = jnp.where(first, grad[:half], grad[half:])
    give_ref[...] = jnp.where(first, grad[half:], grad[:half])
    for at in range(SEG):
        send(at).wait()


def halve_kernel(bit, keep_ref, got_ref, mine_ref, give_ref):
    total = keep_ref[...] + got_ref[...]
    half = total.shape[0] // 2
    first = early(bit)
    mine_ref[...] = jnp.where(first, total[:half], total[half:])
    give_ref[...] = jnp.where(first, total[half:], total[:half])


def join_kernel(own_ref, far_ref, core_ref, both_ref, out_ref):
    rows = own_ref.shape[0]
    place = lax.axis_index("tm")
    low, high = place & 1, (place // 2) & 1
    for ref, a, b in (
        (own_ref, low, high),
        (far_ref, low, 1 - high),
        (core_ref, 1 - low, high),
        (both_ref, 1 - low, 1 - high),
    ):
        out_ref[pl.ds(pl.multiple_of((2 * a + b) * rows, rows), rows), :] = ref[...]


VM = pltpu.VMEM


def call(kernel, name, out, *args, where=None, scratch=(), flops=0, data=0, alias=None):
    where = where or {}
    ins = [pl.BlockSpec(memory_space=pl.ANY if i in where else VM) for i in range(len(args))]
    args = [pltpu.with_memory_space_constraint(a, pltpu.HBM if i in where else VM) for i, a in enumerate(args)]
    outs = tuple(
        pl.BlockSpec(memory_space=pl.ANY if isinstance(o, jax.ShapeDtypeStruct) and len(o.shape) > 2 else VM)
        for o in out
    )
    return pl.pallas_call(
        kernel,
        out_shape=tuple(out),
        in_specs=ins,
        out_specs=outs,
        scratch_shapes=list(scratch),
        input_output_aliases=alias or {},
        compiler_params=pltpu.CompilerParams(vmem_limit_bytes=VMEM_LIMIT),
        cost_estimate=pl.CostEstimate(flops=flops, bytes_accessed=data, transcendentals=0),
        name=name,
    )(*args)


def build(gen, derivs, force):
    steps, width = derivs.shape
    cols = force.shape[1]
    rows = width + cols
    return call(
        build_kernel,
        "build",
        (
            VM((rows, width), F32),
            VM((steps // SEG, rows, width), F32),
            VM((CHUNKS - 1, rows, width), F32),
            VM((2, width, width), BF16),
            VM(derivs.shape, F32),
            VM(force.shape, BF16),
        ),
        gen,
        derivs,
        force,
        where={0, 1, 2},
        scratch=[VM(gen.shape, F32), pltpu.SemaphoreType.DMA((3,))],
        flops=6 * steps * rows * width * width,
    )


def mark_maps(raw, suffix, ins, through):
    count, rows, width = raw.shape
    steps, cols, feats = ins.shape
    return call(
        marks_kernel,
        "marks",
        (
            VM((count, width, width), BF16),
            VM((count, width, width), BF16),
            VM((count, rows - width, width), F32),
            VM((SEG, feats, steps // SEG * cols), BF16),
            VM(through.shape, F32),
        ),
        raw,
        suffix,
        ins,
        through,
        alias={3: 4},
        where={2},
        scratch=[VM(ins.shape, BF16), pltpu.SemaphoreType.DMA],
        flops=6 * count * rows * width * width,
        data=15_000_000,
    )


def sweep(entering, later, zh, zl, zu, rot, derivs, force, flipped):
    steps, cols, width = force.shape
    feats = flipped.shape[1]
    segs = steps // SEG
    adj, keep, give = call(
        functools.partial(sweep_kernel, lax.axis_size("tm") // 2),
        "sweep",
        (
            shape((segs, SEG, cols, width), BF16),
            VM((width // 2, feats), F32),
            VM((width // 2, feats), F32),
        ),
        *entering, later, zh, zl, zu, rot, derivs, force, flipped,
        scratch=[
            VM((segs, cols, width), F32),
            VM((SEG, segs, cols, width), BF16),
            pltpu.SemaphoreType.DMA((SEG,)),
        ],
        flops=8 * steps * cols * width * width,
    )
    return adj.reshape(steps, cols, width), keep, give


def shape(dims, kind=F32):
    return jax.ShapeDtypeStruct(dims, kind)


def swap(x, bit):
    n = lax.axis_size("tm")
    return lax.ppermute(x, "tm", [(i, i ^ bit) for i in range(n)])


def incoming(own, end, aside):
    n = lax.axis_size("tm")
    rows, width = own.shape
    flops = 6 * rows * width * width
    vec = VM(end.shape, F32)
    whole = VM(own.shape, F32)
    half = VM((rows // 2, width), F32)
    other = swap(own, 1)
    total, piece = call(pair_kernel, "pair", (whole, half), own, other, flops=flops)
    (later,) = call(functools.partial(first_later_kernel, 1), "later", (whole,), other)
    bit = 2
    while bit < n // 2:
        count = 4 if 4 * bit <= n // 2 else 2
        mine = [swap(piece, mask * bit) for mask in range(1, count)]
        if bit == 2:
            *marks, mine[0] = aside(mine[0])
        halves = [x for got in mine for x in (got, swap(got, 1))]
        maps = [VM((count, rows, width), F32)]
        if count * bit < n // 2:
            total, piece = call(
                functools.partial(total_kernel, bit), "total", (whole, half), total, *halves,
                scratch=maps, flops=count * flops,
            )
        else:
            (top,) = call(
                functools.partial(top_kernel, bit), "top", (vec,), total, end, *halves,
                scratch=maps, flops=count * flops // 5,
            )
        (later,) = call(
            functools.partial(later_kernel, bit), "later", (whole,), later, *halves,
            scratch=maps, flops=count * flops,
        )
        bit *= count
    return marks, (end, swap(top, n // 2)), later


def all_sum(keep, give):
    n = lax.axis_size("tm")
    quarter = VM((keep.shape[0] // 2, keep.shape[1]), F32)
    mine, give = call(functools.partial(halve_kernel, 2), "halve", (quarter, quarter), keep, swap(give, 1))
    x = mine + swap(give, 2)
    bit = 4
    while bit < n:
        x = x + swap(x, bit)
        bit *= 2
    far = swap(x, 2)
    core = swap(x, 1)
    both = swap(far, 1)
    (out,) = call(join_kernel, "join", (shape((4 * x.shape[0], x.shape[1])),), x, far, core, both)
    return out


def body(generator, derivs, forcing, inputs, terminal):
    force = jnp.transpose(forcing, (0, 2, 1))
    ins = jnp.transpose(inputs, (0, 2, 1))
    end = terminal.T
    own, raw, suffix, rot, derivs, force = build(generator, derivs, force)
    (zh, zl, zu, flipped), entering, later = incoming(own, end, functools.partial(mark_maps, raw, suffix, ins))
    adj, keep, give = sweep(entering, later, zh, zl, zu, rot, derivs, force, flipped)
    return jnp.transpose(adj, (0, 2, 1)), all_sum(keep, give)


def solution(mesh):
    in_specs = (
        P(),
        P(("groups", "tm"), None),
        P(("groups", "tm"), None, None),
        P(("groups", "tm"), None, None),
        P("groups", None),
    )
    out_specs = (P(("groups", "tm"), None, None), P("groups", None))
    return jax.shard_map(body, mesh=mesh, in_specs=in_specs, out_specs=out_specs, check_vma=False)
```

```python
import functools
import math

import jax
import jax.numpy as jnp
from jax import lax
from jax.experimental import pallas as pl
from jax.experimental.pallas import tpu as pltpu
from jax.sharding import PartitionSpec as P

F32 = jnp.float32
BF16 = jnp.bfloat16
VMEM_LIMIT = 24 * 1024 * 1024
CHUNKS = 4
SEG = 8


def mm(a, b):
    return jnp.dot(a, b, preferred_element_type=F32)


def split(x):
    high = x.astype(BF16)
    low = (x - high.astype(F32)).astype(BF16)
    return high, low


def mm3(a, b_high, b_low):
    a_high, a_low = split(a)
    return mm(a_high, b_high) + mm(a_low, b_high) + mm(a_high, b_low)


def rotation(gen):
    n = gen.shape[0]
    skew = gen - gen.T
    ident = (
        lax.broadcasted_iota(jnp.int32, (n, n), 0) == lax.broadcasted_iota(jnp.int32, (n, n), 1)
    ).astype(F32)
    c = [1.0 / math.factorial(k) for k in range(13)]
    halves = split(skew)
    s2 = mm3(skew, *halves)
    s3 = mm3(s2, *halves)
    s4 = mm3(s2, *split(s2))
    top = c[8] * ident + c[9] * skew + c[10] * s2 + c[11] * s3 + c[12] * s4
    mid = c[4] * ident + c[5] * skew + c[6] * s2 + c[7] * s3
    bottom = ident + skew + c[2] * s2 + c[3] * s3
    inner = mid + mm3(s4, *split(top))
    return bottom + mm3(s4, *split(inner))


def compose(rows_in, through, width):
    high, low = split(through[:width])
    out = mm3(rows_in, high, low)
    return jnp.concatenate([out[:width], out[width:] + through[width:]], axis=0)


def apply(vec, through, width):
    high, low = split(through[:width])
    return mm3(vec, high, low) + through[width:]


def build_kernel(gen_hbm, d_hbm, f_hbm, map_ref, raw_ref, rot_ref, d_ref, f_ref, gen_ref, sems):
    steps, width = d_ref.shape
    per = steps // CHUNKS
    marks = per // SEG
    fetches = [
        pltpu.make_async_copy(far, here, sems.at[i])
        for i, (far, here) in enumerate(((gen_hbm, gen_ref), (d_hbm, d_ref), (f_hbm, f_ref)))
    ]
    for fetch in fetches:
        fetch.start()
    fetches[0].wait()
    rot = rotation(gen_ref[...])
    rot_high, rot_low = split(rot)
    rot_ref[0] = rot_high
    rot_ref[1] = rot_low
    fetches[1].wait()
    fetches[2].wait()

    def run(k, states, done):
        for s in range(done, SEG):
            out = []
            for g in range(CHUNKS):
                t = g * per + per - 1 - k * SEG - s
                moved = mm3(states[g] * d_ref[pl.ds(t, 1), :], rot_ref[0], rot_ref[1])
                out.append(
                    jnp.concatenate([moved[:width], moved[width:] + f_ref[t].astype(F32)], axis=0)
                )
            states = out
        for g in range(CHUNKS):
            raw_ref[g * marks + marks - 1 - k] = states[g]

    first = []
    for g in range(CHUNKS):
        end = (g + 1) * per
        column = d_ref[end - 8 : end, :].T[:, 7:8]
        first.append(jnp.concatenate([rot * column, f_ref[end - 1].astype(F32)], axis=0))
    run(0, first, 1)

    def more(k, _):
        run(k, [raw_ref[g * marks + marks - k] for g in range(CHUNKS)], 0)
        return 0

    lax.fori_loop(1, marks, more, 0)
    maps = [raw_ref[g * marks] for g in range(CHUNKS)]
    while len(maps) > 1:
        maps = [compose(maps[i + 1], maps[i], width) for i in range(0, len(maps), 2)]
    map_ref[...] = maps[0]


def marks_kernel(raw_ref, in_hbm, _, zh_ref, zl_ref, zu_ref, flip_ref, __, in_ref, sem):
    fetch = pltpu.make_async_copy(in_hbm, in_ref, sem)
    fetch.start()
    count, rows, width = raw_ref.shape
    marks = count // CHUNKS
    suffix = None
    for g in range(CHUNKS - 1, -1, -1):
        for j in range((g + 1) * marks - 1, g * marks - 1, -1):
            full = raw_ref[j]
            if suffix is not None:
                full = compose(suffix, full, width)
            high, low = split(full[:width])
            zh_ref[j] = high
            zl_ref[j] = low
            zu_ref[j] = full[width:]
        suffix = full
    fetch.wait()
    segs = in_ref.shape[0] // SEG
    for s in range(SEG):
        block = jnp.concatenate([in_ref[m * SEG + s] for m in range(segs)], axis=0)
        flip_ref[s] = block.T


def early(bit):
    return (lax.axis_index("tm") & bit) == 0


def core_half(ref):
    half = ref.shape[0] // 2
    return ref[pl.ds(pl.multiple_of((lax.axis_index("tm") & 1) * half, half), half), :]


def place_halves(mine, other, out_ref):
    half = mine.shape[0]
    start = pl.multiple_of((lax.axis_index("tm") & 1) * half, half)
    out_ref[pl.ds(start, half), :] = mine
    out_ref[pl.ds(pl.multiple_of(half - start, half), half), :] = other


def ordered(bit, own_ref, other_ref, out_ref):
    width = own_ref.shape[1]
    first = early(bit)

    @pl.when(first)
    def _():
        out_ref[...] = compose(other_ref[...], own_ref[...], width)

    @pl.when(jnp.logical_not(first))
    def _():
        out_ref[...] = compose(own_ref[...], other_ref[...], width)


def pair_kernel(own_ref, other_ref, out_ref, half_ref):
    ordered(1, own_ref, other_ref, out_ref)
    half_ref[...] = core_half(out_ref)


def position(low_bit, count):
    return (lax.axis_index("tm") // low_bit) % count


def group_maps(own_ref, halves, maps):
    maps[0] = own_ref[...]
    for mask in range(1, maps.shape[0]):
        place_halves(halves[2 * mask - 2][...], halves[2 * mask - 1][...], maps.at[mask])


def top_kernel(low_bit, own_ref, vec_ref, *rest):
    halves, (out_ref, maps) = rest[:-2], rest[-2:]
    group_maps(own_ref, halves, maps)
    count, _, width = maps.shape
    here = position(low_bit, count)
    vec = vec_ref[...]
    for at in range(count - 1, -1, -1):
        vec = apply(vec, maps[at ^ here], width)
    out_ref[...] = vec


def total_kernel(low_bit, own_ref, *rest):
    halves, (out_ref, half_ref, maps) = rest[:-3], rest[-3:]
    group_maps(own_ref, halves, maps)
    count, _, width = maps.shape
    here = position(low_bit, count)
    acc = maps[(count - 1) ^ here]
    for at in range(count - 2, -1, -1):
        acc = compose(acc, maps[at ^ here], width)
    out_ref[...] = acc
    half_ref[...] = core_half(out_ref)


def later_kernel(low_bit, later_ref, *rest):
    halves, (out_ref, maps) = rest[:-2], rest[-2:]
    count, _, width = maps.shape
    for mask in range(1, count):
        place_halves(halves[2 * mask - 2][...], halves[2 * mask - 1][...], maps.at[mask])
    here = position(low_bit, count)
    maps[0] = later_ref[...]
    out_ref[...] = maps[jnp.where(here == count - 1, 0, (count - 1) ^ here)]
    for at in range(count - 2, -1, -1):

        @pl.when(at >= here)
        def _():
            out_ref[...] = compose(out_ref[...], maps[at ^ here], width)


def first_later_kernel(bit, other_ref, out_ref):
    rows, width = other_ref.shape
    first = early(bit)

    @pl.when(first)
    def _():
        out_ref[...] = other_ref[...]

    @pl.when(jnp.logical_not(first))
    def _():
        out_ref[...] = (
            lax.broadcasted_iota(jnp.int32, (rows, width), 0) == lax.broadcasted_iota(jnp.int32, (rows, width), 1)
        ).astype(F32)


def sweep_kernel(
    bit, end_ref, got_ref, later_ref, zh_ref, zl_ref, zu_ref,
    rot_ref, d_ref, f_ref, flip_ref,
    adj_hbm, keep_ref, give_ref, cur, low_ref, sems,
):
    count, width = zh_ref.shape[0], zh_ref.shape[1]
    cols = end_ref.shape[0]
    v = jnp.where(early(bit), got_ref[...], end_ref[...])
    v = apply(v, later_ref[...], width)
    v_high, v_low = split(v)
    v_both = jnp.concatenate([v_high, v_low], axis=0)

    def send(at):
        return pltpu.make_async_copy(low_ref.at[at], adj_hbm.at[:, at], sems.at[at])

    for j in range(count):
        both = mm(v_both, zh_ref[j])
        z = both[:cols] + both[cols:] + mm(v_high, zl_ref[j]) + zu_ref[j]
        if j > 0:
            cur[j - 1] = z
        low_ref[0, j] = z.astype(BF16)
    cur[count - 1] = v
    send(0).start()
    grad = mm(flip_ref[0], low_ref[0].reshape(count * cols, width))
    pack = 4
    for s in range(SEG - 1):
        at = SEG - 1 - s
        for p in range(0, count, pack):
            scaled = jnp.concatenate(
                [cur[m] * d_ref[m * SEG + at : m * SEG + at + 1, :] for m in range(p, p + pack)], axis=0
            )
            out = mm3(scaled, rot_ref[0], rot_ref[1])
            for m in range(p, p + pack):
                value = out[(m - p) * cols : (m - p + 1) * cols] + f_ref[m * SEG + at].astype(F32)
                cur[m] = value
                low_ref[at, m] = value.astype(BF16)
        send(at).start()
        grad = grad + mm(flip_ref[at], low_ref[at].reshape(count * cols, width))
    grad = grad.T
    half = width // 2
    first = early(1)
    keep_ref[...] = jnp.where(first, grad[:half], grad[half:])
    give_ref[...] = jnp.where(first, grad[half:], grad[:half])
    for at in range(SEG):
        send(at).wait()


def halve_kernel(bit, keep_ref, got_ref, mine_ref, give_ref):
    total = keep_ref[...] + got_ref[...]
    half = total.shape[0] // 2
    first = early(bit)
    mine_ref[...] = jnp.where(first, total[:half], total[half:])
    give_ref[...] = jnp.where(first, total[half:], total[:half])


def join_kernel(bit, own_ref, far_ref, core_ref, both_ref, out_ref):
    rows = own_ref.shape[0]
    place = lax.axis_index("tm")
    low, high = place & 1, (place // bit) & 1
    for ref, a, b in (
        (own_ref, low, high),
        (far_ref, low, 1 - high),
        (core_ref, 1 - low, high),
        (both_ref, 1 - low, 1 - high),
    ):
        out_ref[pl.ds(pl.multiple_of((2 * a + b) * rows, rows), rows), :] = ref[...]


VM = pltpu.VMEM


def call(kernel, name, out, *args, where=None, scratch=(), flops=0, data=0, alias=None):
    where = where or {}
    ins = [pl.BlockSpec(memory_space=pl.ANY if i in where else VM) for i in range(len(args))]
    args = [pltpu.with_memory_space_constraint(a, pltpu.HBM if i in where else VM) for i, a in enumerate(args)]
    outs = tuple(
        pl.BlockSpec(memory_space=pl.ANY if isinstance(o, jax.ShapeDtypeStruct) and len(o.shape) > 2 else VM)
        for o in out
    )
    return pl.pallas_call(
        kernel,
        out_shape=tuple(out),
        in_specs=ins,
        out_specs=outs,
        scratch_shapes=list(scratch),
        input_output_aliases=alias or {},
        compiler_params=pltpu.CompilerParams(vmem_limit_bytes=VMEM_LIMIT),
        cost_estimate=pl.CostEstimate(flops=flops, bytes_accessed=data, transcendentals=0),
        name=name,
    )(*args)


def build(gen, derivs, force):
    steps, width = derivs.shape
    cols = force.shape[1]
    rows = width + cols
    return call(
        build_kernel,
        "build",
        (
            VM((rows, width), F32),
            VM((steps // SEG, rows, width), F32),
            VM((2, width, width), BF16),
            VM(derivs.shape, F32),
            VM(force.shape, BF16),
        ),
        gen,
        derivs,
        force,
        where={0, 1, 2},
        scratch=[VM(gen.shape, F32), pltpu.SemaphoreType.DMA((3,))],
        flops=6 * steps * rows * width * width,
    )


def mark_maps(raw, ins, through):
    count, rows, width = raw.shape
    steps, cols, feats = ins.shape
    return call(
        marks_kernel,
        "marks",
        (
            VM((count, width, width), BF16),
            VM((count, width, width), BF16),
            VM((count, rows - width, width), F32),
            VM((SEG, feats, steps // SEG * cols), BF16),
            VM(through.shape, F32),
        ),
        raw,
        ins,
        through,
        alias={2: 4},
        where={1},
        scratch=[VM(ins.shape, BF16), pltpu.SemaphoreType.DMA],
        flops=6 * count * rows * width * width,
        data=15_000_000,
    )


def sweep(entering, later, zh, zl, zu, rot, derivs, force, flipped):
    steps, cols, width = force.shape
    feats = flipped.shape[1]
    segs = steps // SEG
    adj, keep, give = call(
        functools.partial(sweep_kernel, lax.axis_size("tm") // 2),
        "sweep",
        (
            shape((segs, SEG, cols, width), BF16),
            VM((width // 2, feats), F32),
            VM((width // 2, feats), F32),
        ),
        *entering, later, zh, zl, zu, rot, derivs, force, flipped,
        scratch=[
            VM((segs, cols, width), F32),
            VM((SEG, segs, cols, width), BF16),
            pltpu.SemaphoreType.DMA((SEG,)),
        ],
        flops=8 * steps * cols * width * width,
    )
    return adj.reshape(steps, cols, width), keep, give


def shape(dims, kind=F32):
    return jax.ShapeDtypeStruct(dims, kind)


def swap(x, bit):
    n = lax.axis_size("tm")
    return lax.ppermute(x, "tm", [(i, i ^ bit) for i in range(n)])


def incoming(own, end, aside):
    n = lax.axis_size("tm")
    rows, width = own.shape
    flops = 6 * rows * width * width
    vec = VM(end.shape, F32)
    whole = VM(own.shape, F32)
    half = VM((rows // 2, width), F32)
    other = swap(own, 1)
    total, piece = call(pair_kernel, "pair", (whole, half), own, other, flops=flops)
    (later,) = call(functools.partial(first_later_kernel, 1), "later", (whole,), other)
    bit = 2
    while bit < n // 2:
        count = 4 if 4 * bit <= n // 2 else 2
        mine = [swap(piece, mask * bit) for mask in range(1, count)]
        if bit == 2:
            *marks, mine[0] = aside(mine[0])
        halves = [x for got in mine for x in (got, swap(got, 1))]
        maps = [VM((count, rows, width), F32)]
        if count * bit < n // 2:
            total, piece = call(
                functools.partial(total_kernel, bit), "total", (whole, half), total, *halves,
                scratch=maps, flops=count * flops,
            )
        else:
            (top,) = call(
                functools.partial(top_kernel, bit), "top", (vec,), total, end, *halves,
                scratch=maps, flops=count * flops // 5,
            )
        (later,) = call(
            functools.partial(later_kernel, bit), "later", (whole,), later, *halves,
            scratch=maps, flops=count * flops,
        )
        bit *= count
    return marks, (end, swap(top, n // 2)), later


def all_sum(keep, give):
    n = lax.axis_size("tm")
    near = 2
    quarter = VM((keep.shape[0] // 2, keep.shape[1]), F32)
    x, give = call(functools.partial(halve_kernel, near), "halve", (quarter, quarter), keep, swap(give, 1))
    x = x + swap(give, near)
    bit = 2 * near
    while bit < n:
        count = 4 if 4 * bit <= n else 2
        others = [swap(x, mask * bit) for mask in range(1, count)]
        x = sum(others, x)
        bit *= count
    far = swap(x, near)
    core = swap(x, 1)
    both = swap(far, 1)
    (out,) = call(
        functools.partial(join_kernel, near), "join", (shape((4 * x.shape[0], x.shape[1])),), x, far, core, both
    )
    return out


def body(generator, derivs, forcing, inputs, terminal):
    force = jnp.transpose(forcing, (0, 2, 1))
    ins = jnp.transpose(inputs, (0, 2, 1))
    end = terminal.T
    own, raw, rot, derivs, force = build(generator, derivs, force)
    (zh, zl, zu, flipped), entering, later = incoming(own, end, functools.partial(mark_maps, raw, ins))
    adj, keep, give = sweep(entering, later, zh, zl, zu, rot, derivs, force, flipped)
    return jnp.transpose(adj, (0, 2, 1)), all_sum(keep, give)


def solution(mesh):
    in_specs = (
        P(),
        P(("groups", "tm"), None),
        P(("groups", "tm"), None, None),
        P(("groups", "tm"), None, None),
        P("groups", None),
    )
    out_specs = (P(("groups", "tm"), None, None), P("groups", None))
    return jax.shard_map(body, mesh=mesh, in_specs=in_specs, out_specs=out_specs, check_vma=False)
```

```python
import functools
import math

import jax
import jax.numpy as jnp
from jax import lax
from jax.experimental import pallas as pl
from jax.experimental.pallas import tpu as pltpu
from jax.sharding import PartitionSpec as P

F32 = jnp.float32
BF16 = jnp.bfloat16
F8 = jnp.float8_e4m3fn
LIFT = 4096.0
VMEM_LIMIT = 24 * 1024 * 1024
CHUNKS = 4
SEG = 8


def mm(a, b):
    return jnp.dot(a, b, preferred_element_type=F32)


def split(x):
    high = x.astype(BF16)
    low = (x - high.astype(F32)).astype(BF16)
    return high, low


def mm3(a, b_high, b_low):
    a_high, a_low = split(a)
    return mm(a_high, b_high) + mm(a_low, b_high) + mm(a_high, b_low)


def rotation(gen):
    n = gen.shape[0]
    skew = gen - gen.T
    ident = (
        lax.broadcasted_iota(jnp.int32, (n, n), 0) == lax.broadcasted_iota(jnp.int32, (n, n), 1)
    ).astype(F32)
    c = [1.0 / math.factorial(k) for k in range(13)]
    halves = split(skew)
    s2 = mm3(skew, *halves)
    s3 = mm3(s2, *halves)
    s4 = mm3(s2, *split(s2))
    top = c[8] * ident + c[9] * skew + c[10] * s2 + c[11] * s3 + c[12] * s4
    mid = c[4] * ident + c[5] * skew + c[6] * s2 + c[7] * s3
    bottom = ident + skew + c[2] * s2 + c[3] * s3
    inner = mid + mm3(s4, *split(top))
    return bottom + mm3(s4, *split(inner))


def step_rows(x, width, rot_ref, coarse_ref):
    rows = x.shape[0]
    high = x.astype(BF16)
    low = x - high.astype(F32)
    both = mm(jnp.concatenate([high, low[width:].astype(BF16)], axis=0), rot_ref[0])
    fine = mm(high, rot_ref[1])
    small = mm((low[:width] * LIFT).astype(F8), coarse_ref[...]) * (1.0 / LIFT)
    return jnp.concatenate(
        [both[:width] + fine[:width] + small, both[width:rows] + fine[width:] + both[rows:]], axis=0
    )


def compose(rows_in, through, width):
    high, low = split(through[:width])
    out = mm3(rows_in, high, low)
    return jnp.concatenate([out[:width], out[width:] + through[width:]], axis=0)


def apply(vec, through, width):
    high, low = split(through[:width])
    return mm3(vec, high, low) + through[width:]


def build_kernel(gen_hbm, d_hbm, f_hbm, map_ref, raw_ref, rot_ref, d_ref, f_ref, gen_ref, coarse_ref, sems):
    steps, width = d_ref.shape
    per = steps // CHUNKS
    marks = per // SEG
    fetches = [
        pltpu.make_async_copy(far, here, sems.at[i])
        for i, (far, here) in enumerate(((gen_hbm, gen_ref), (d_hbm, d_ref), (f_hbm, f_ref)))
    ]
    for fetch in fetches:
        fetch.start()
    fetches[0].wait()
    rot = rotation(gen_ref[...])
    rot_high, rot_low = split(rot)
    rot_ref[0] = rot_high
    rot_ref[1] = rot_low
    coarse_ref[...] = rot.astype(F8)
    fetches[1].wait()
    fetches[2].wait()

    def run(k, states, done):
        for s in range(done, SEG):
            out = []
            for g in range(CHUNKS):
                t = g * per + per - 1 - k * SEG - s
                moved = step_rows(states[g] * d_ref[pl.ds(t, 1), :], width, rot_ref, coarse_ref)
                out.append(
                    jnp.concatenate([moved[:width], moved[width:] + f_ref[t].astype(F32)], axis=0)
                )
            states = out
        for g in range(CHUNKS):
            raw_ref[g * marks + marks - 1 - k] = states[g]

    first = []
    for g in range(CHUNKS):
        end = (g + 1) * per
        column = d_ref[end - 8 : end, :].T[:, 7:8]
        first.append(jnp.concatenate([rot * column, f_ref[end - 1].astype(F32)], axis=0))
    run(0, first, 1)

    def more(k, _):
        run(k, [raw_ref[g * marks + marks - k] for g in range(CHUNKS)], 0)
        return 0

    lax.fori_loop(1, marks, more, 0)
    maps = [raw_ref[g * marks] for g in range(CHUNKS)]
    while len(maps) > 1:
        maps = [compose(maps[i + 1], maps[i], width) for i in range(0, len(maps), 2)]
    map_ref[...] = maps[0]


def marks_kernel(raw_ref, in_hbm, _, zh_ref, zl_ref, zu_ref, flip_ref, __, in_ref, sem):
    fetch = pltpu.make_async_copy(in_hbm, in_ref, sem)
    fetch.start()
    count, rows, width = raw_ref.shape
    marks = count // CHUNKS
    suffix = None
    for g in range(CHUNKS - 1, -1, -1):
        for j in range((g + 1) * marks - 1, g * marks - 1, -1):
            full = raw_ref[j]
            if suffix is not None:
                full = compose(suffix, full, width)
            high, low = split(full[:width])
            zh_ref[j] = high
            zl_ref[j] = low
            zu_ref[j] = full[width:]
        suffix = full
    fetch.wait()
    segs = in_ref.shape[0] // SEG
    for s in range(SEG):
        block = jnp.concatenate([in_ref[m * SEG + s] for m in range(segs)], axis=0)
        flip_ref[s] = block.T


def early(bit):
    return (lax.axis_index("tm") & bit) == 0


def core_half(ref):
    half = ref.shape[0] // 2
    return ref[pl.ds(pl.multiple_of((lax.axis_index("tm") & 1) * half, half), half), :]


def place_halves(mine, other, out_ref):
    half = mine.shape[0]
    start = pl.multiple_of((lax.axis_index("tm") & 1) * half, half)
    out_ref[pl.ds(start, half), :] = mine
    out_ref[pl.ds(pl.multiple_of(half - start, half), half), :] = other


def ordered(bit, own_ref, other_ref, out_ref):
    width = own_ref.shape[1]
    first = early(bit)

    @pl.when(first)
    def _():
        out_ref[...] = compose(other_ref[...], own_ref[...], width)

    @pl.when(jnp.logical_not(first))
    def _():
        out_ref[...] = compose(own_ref[...], other_ref[...], width)


def pair_kernel(own_ref, other_ref, out_ref, half_ref):
    ordered(1, own_ref, other_ref, out_ref)
    half_ref[...] = core_half(out_ref)


def position(low_bit, count):
    return (lax.axis_index("tm") // low_bit) % count


def group_maps(own_ref, halves, maps):
    maps[0] = own_ref[...]
    for mask in range(1, maps.shape[0]):
        place_halves(halves[2 * mask - 2][...], halves[2 * mask - 1][...], maps.at[mask])


def top_kernel(low_bit, own_ref, vec_ref, *rest):
    halves, (out_ref, maps) = rest[:-2], rest[-2:]
    group_maps(own_ref, halves, maps)
    count, _, width = maps.shape
    here = position(low_bit, count)
    vec = vec_ref[...]
    for at in range(count - 1, -1, -1):
        vec = apply(vec, maps[at ^ here], width)
    out_ref[...] = vec


def total_kernel(low_bit, own_ref, *rest):
    halves, (out_ref, half_ref, maps) = rest[:-3], rest[-3:]
    group_maps(own_ref, halves, maps)
    count, _, width = maps.shape
    here = position(low_bit, count)
    acc = maps[(count - 1) ^ here]
    for at in range(count - 2, -1, -1):
        acc = compose(acc, maps[at ^ here], width)
    out_ref[...] = acc
    half_ref[...] = core_half(out_ref)


def later_kernel(low_bit, later_ref, *rest):
    halves, (out_ref, maps) = rest[:-2], rest[-2:]
    count, _, width = maps.shape
    for mask in range(1, count):
        place_halves(halves[2 * mask - 2][...], halves[2 * mask - 1][...], maps.at[mask])
    here = position(low_bit, count)
    maps[0] = later_ref[...]
    out_ref[...] = maps[jnp.where(here == count - 1, 0, (count - 1) ^ here)]
    for at in range(count - 2, -1, -1):

        @pl.when(at >= here)
        def _():
            out_ref[...] = compose(out_ref[...], maps[at ^ here], width)


def first_later_kernel(bit, other_ref, out_ref):
    rows, width = other_ref.shape
    first = early(bit)

    @pl.when(first)
    def _():
        out_ref[...] = other_ref[...]

    @pl.when(jnp.logical_not(first))
    def _():
        out_ref[...] = (
            lax.broadcasted_iota(jnp.int32, (rows, width), 0) == lax.broadcasted_iota(jnp.int32, (rows, width), 1)
        ).astype(F32)


def sweep_kernel(
    bit, end_ref, got_ref, later_ref, zh_ref, zl_ref, zu_ref,
    rot_ref, d_ref, f_ref, flip_ref,
    adj_hbm, keep_ref, give_ref, cur, low_ref, sems,
):
    count, width = zh_ref.shape[0], zh_ref.shape[1]
    cols = end_ref.shape[0]
    v = jnp.where(early(bit), got_ref[...], end_ref[...])
    v = apply(v, later_ref[...], width)
    v_high, v_low = split(v)
    v_both = jnp.concatenate([v_high, v_low], axis=0)

    def send(at):
        return pltpu.make_async_copy(low_ref.at[at], adj_hbm.at[:, at], sems.at[at])

    for j in range(count):
        both = mm(v_both, zh_ref[j])
        z = both[:cols] + both[cols:] + mm(v_high, zl_ref[j]) + zu_ref[j]
        if j > 0:
            cur[j - 1] = z
        low_ref[0, j] = z.astype(BF16)
    cur[count - 1] = v
    send(0).start()
    grad = mm(flip_ref[0], low_ref[0].reshape(count * cols, width))
    pack = 4
    for s in range(SEG - 1):
        at = SEG - 1 - s
        for p in range(0, count, pack):
            scaled = jnp.concatenate(
                [cur[m] * d_ref[m * SEG + at : m * SEG + at + 1, :] for m in range(p, p + pack)], axis=0
            )
            out = mm3(scaled, rot_ref[0], rot_ref[1])
            for m in range(p, p + pack):
                value = out[(m - p) * cols : (m - p + 1) * cols] + f_ref[m * SEG + at].astype(F32)
                cur[m] = value
                low_ref[at, m] = value.astype(BF16)
        send(at).start()
        grad = grad + mm(flip_ref[at], low_ref[at].reshape(count * cols, width))
    grad = grad.T
    half = width // 2
    first = early(1)
    keep_ref[...] = jnp.where(first, grad[:half], grad[half:])
    give_ref[...] = jnp.where(first, grad[half:], grad[:half])
    for at in range(SEG):
        send(at).wait()


def halve_kernel(bit, keep_ref, got_ref, mine_ref, give_ref):
    total = keep_ref[...] + got_ref[...]
    half = total.shape[0] // 2
    first = early(bit)
    mine_ref[...] = jnp.where(first, total[:half], total[half:])
    give_ref[...] = jnp.where(first, total[half:], total[:half])


def join_kernel(bit, own_ref, far_ref, core_ref, both_ref, out_ref):
    rows = own_ref.shape[0]
    place = lax.axis_index("tm")
    low, high = place & 1, (place // bit) & 1
    for ref, a, b in (
        (own_ref, low, high),
        (far_ref, low, 1 - high),
        (core_ref, 1 - low, high),
        (both_ref, 1 - low, 1 - high),
    ):
        out_ref[pl.ds(pl.multiple_of((2 * a + b) * rows, rows), rows), :] = ref[...]


VM = pltpu.VMEM


def call(kernel, name, out, *args, where=None, scratch=(), flops=0, data=0, alias=None):
    where = where or {}
    ins = [pl.BlockSpec(memory_space=pl.ANY if i in where else VM) for i in range(len(args))]
    args = [pltpu.with_memory_space_constraint(a, pltpu.HBM if i in where else VM) for i, a in enumerate(args)]
    outs = tuple(
        pl.BlockSpec(memory_space=pl.ANY if isinstance(o, jax.ShapeDtypeStruct) and len(o.shape) > 2 else VM)
        for o in out
    )
    return pl.pallas_call(
        kernel,
        out_shape=tuple(out),
        in_specs=ins,
        out_specs=outs,
        scratch_shapes=list(scratch),
        input_output_aliases=alias or {},
        compiler_params=pltpu.CompilerParams(vmem_limit_bytes=VMEM_LIMIT),
        cost_estimate=pl.CostEstimate(flops=flops, bytes_accessed=data, transcendentals=0),
        name=name,
    )(*args)


def build(gen, derivs, force):
    steps, width = derivs.shape
    cols = force.shape[1]
    rows = width + cols
    return call(
        build_kernel,
        "build",
        (
            VM((rows, width), F32),
            VM((steps // SEG, rows, width), F32),
            VM((2, width, width), BF16),
            VM(derivs.shape, F32),
            VM(force.shape, BF16),
        ),
        gen,
        derivs,
        force,
        where={0, 1, 2},
        scratch=[VM(gen.shape, F32), VM(gen.shape, F8), pltpu.SemaphoreType.DMA((3,))],
        flops=6 * steps * rows * width * width,
    )


def mark_maps(raw, ins, through):
    count, rows, width = raw.shape
    steps, cols, feats = ins.shape
    return call(
        marks_kernel,
        "marks",
        (
            VM((count, width, width), BF16),
            VM((count, width, width), BF16),
            VM((count, rows - width, width), F32),
            VM((SEG, feats, steps // SEG * cols), BF16),
            VM(through.shape, F32),
        ),
        raw,
        ins,
        through,
        alias={2: 4},
        where={1},
        scratch=[VM(ins.shape, BF16), pltpu.SemaphoreType.DMA],
        flops=6 * count * rows * width * width,
        data=15_000_000,
    )


def sweep(entering, later, zh, zl, zu, rot, derivs, force, flipped):
    steps, cols, width = force.shape
    feats = flipped.shape[1]
    segs = steps // SEG
    adj, keep, give = call(
        functools.partial(sweep_kernel, lax.axis_size("tm") // 2),
        "sweep",
        (
            shape((segs, SEG, cols, width), BF16),
            VM((width // 2, feats), F32),
            VM((width // 2, feats), F32),
        ),
        *entering, later, zh, zl, zu, rot, derivs, force, flipped,
        scratch=[
            VM((segs, cols, width), F32),
            VM((SEG, segs, cols, width), BF16),
            pltpu.SemaphoreType.DMA((SEG,)),
        ],
        flops=8 * steps * cols * width * width,
    )
    return adj.reshape(steps, cols, width), keep, give


def shape(dims, kind=F32):
    return jax.ShapeDtypeStruct(dims, kind)


def swap(x, bit):
    n = lax.axis_size("tm")
    return lax.ppermute(x, "tm", [(i, i ^ bit) for i in range(n)])


def incoming(own, end, aside):
    n = lax.axis_size("tm")
    rows, width = own.shape
    flops = 6 * rows * width * width
    vec = VM(end.shape, F32)
    whole = VM(own.shape, F32)
    half = VM((rows // 2, width), F32)
    other = swap(own, 1)
    total, piece = call(pair_kernel, "pair", (whole, half), own, other, flops=flops)
    (later,) = call(functools.partial(first_later_kernel, 1), "later", (whole,), other)
    bit = 2
    while bit < n // 2:
        count = 4 if 4 * bit <= n // 2 else 2
        mine = [swap(piece, mask * bit) for mask in range(1, count)]
        if bit == 2:
            *marks, mine[0] = aside(mine[0])
        halves = [x for got in mine for x in (got, swap(got, 1))]
        maps = [VM((count, rows, width), F32)]
        if count * bit < n // 2:
            total, piece = call(
                functools.partial(total_kernel, bit), "total", (whole, half), total, *halves,
                scratch=maps, flops=count * flops,
            )
        else:
            (top,) = call(
                functools.partial(top_kernel, bit), "top", (vec,), total, end, *halves,
                scratch=maps, flops=count * flops // 5,
            )
        (later,) = call(
            functools.partial(later_kernel, bit), "later", (whole,), later, *halves,
            scratch=maps, flops=count * flops,
        )
        bit *= count
    return marks, (end, swap(top, n // 2)), later


def all_sum(keep, give):
    n = lax.axis_size("tm")
    near = 2
    quarter = VM((keep.shape[0] // 2, keep.shape[1]), F32)
    x, give = call(functools.partial(halve_kernel, near), "halve", (quarter, quarter), keep, swap(give, 1))
    x = x + swap(give, near)
    bit = 2 * near
    while bit < n:
        count = 4 if 4 * bit <= n else 2
        others = [swap(x, mask * bit) for mask in range(1, count)]
        x = sum(others, x)
        bit *= count
    far = swap(x, near)
    core = swap(x, 1)
    both = swap(far, 1)
    (out,) = call(
        functools.partial(join_kernel, near), "join", (shape((4 * x.shape[0], x.shape[1])),), x, far, core, both
    )
    return out


def body(generator, derivs, forcing, inputs, terminal):
    force = jnp.transpose(forcing, (0, 2, 1))
    ins = jnp.transpose(inputs, (0, 2, 1))
    end = terminal.T
    own, raw, rot, derivs, force = build(generator, derivs, force)
    (zh, zl, zu, flipped), entering, later = incoming(own, end, functools.partial(mark_maps, raw, ins))
    adj, keep, give = sweep(entering, later, zh, zl, zu, rot, derivs, force, flipped)
    return jnp.transpose(adj, (0, 2, 1)), all_sum(keep, give)


def solution(mesh):
    in_specs = (
        P(),
        P(("groups", "tm"), None),
        P(("groups", "tm"), None, None),
        P(("groups", "tm"), None, None),
        P("groups", None),
    )
    out_specs = (P(("groups", "tm"), None, None), P("groups", None))
    return jax.shard_map(body, mesh=mesh, in_specs=in_specs, out_specs=out_specs, check_vma=False)
```

```python
import functools
import math

import jax
import jax.numpy as jnp
from jax import lax
from jax.experimental import pallas as pl
from jax.experimental.pallas import tpu as pltpu
from jax.sharding import PartitionSpec as P

F32 = jnp.float32
BF16 = jnp.bfloat16
F8 = jnp.float8_e4m3fn
LIFT = 1024.0
F8_MAX = 448.0
VMEM_LIMIT = 24 * 1024 * 1024
CHUNKS = 4
SEG = 8


def mm(a, b):
    return jnp.dot(a, b, preferred_element_type=F32)


def split(x):
    high = x.astype(BF16)
    low = (x - high.astype(F32)).astype(BF16)
    return high, low


def mm3(a, b_high, b_low):
    a_high, a_low = split(a)
    return mm(a_high, b_high) + mm(a_low, b_high) + mm(a_high, b_low)


def rotation(gen):
    n = gen.shape[0]
    skew = gen - gen.T
    ident = (
        lax.broadcasted_iota(jnp.int32, (n, n), 0) == lax.broadcasted_iota(jnp.int32, (n, n), 1)
    ).astype(F32)
    c = [1.0 / math.factorial(k) for k in range(13)]
    halves = split(skew)
    s2 = mm3(skew, *halves)
    s3 = mm3(s2, *halves)
    s4 = mm3(s2, *split(s2))
    top = c[8] * ident + c[9] * skew + c[10] * s2 + c[11] * s3 + c[12] * s4
    mid = c[4] * ident + c[5] * skew + c[6] * s2 + c[7] * s3
    bottom = ident + skew + c[2] * s2 + c[3] * s3
    inner = mid + mm3(s4, *split(top))
    return bottom + mm3(s4, *split(inner))


def step_rows(x, width, rot_ref, coarse_ref):
    rows = x.shape[0]
    high = x.astype(BF16)
    low = x - high.astype(F32)
    both = mm(jnp.concatenate([high, low[width:].astype(BF16)], axis=0), rot_ref[0])
    fine = mm(high, rot_ref[1])
    lifted = jnp.clip(low[:width] * LIFT, -F8_MAX, F8_MAX).astype(F8)
    small = mm(lifted, coarse_ref[...]) * (1.0 / LIFT)
    return jnp.concatenate(
        [both[:width] + fine[:width] + small, both[width:rows] + fine[width:] + both[rows:]], axis=0
    )


def compose(rows_in, through, width):
    high, low = split(through[:width])
    out = mm3(rows_in, high, low)
    return jnp.concatenate([out[:width], out[width:] + through[width:]], axis=0)


def apply(vec, through, width):
    high, low = split(through[:width])
    return mm3(vec, high, low) + through[width:]


def build_kernel(gen_hbm, d_hbm, f_hbm, map_ref, raw_ref, rot_ref, d_ref, f_ref, gen_ref, coarse_ref, sems):
    steps, width = d_ref.shape
    per = steps // CHUNKS
    marks = per // SEG
    fetches = [
        pltpu.make_async_copy(far, here, sems.at[i])
        for i, (far, here) in enumerate(((gen_hbm, gen_ref), (d_hbm, d_ref), (f_hbm, f_ref)))
    ]
    for fetch in fetches:
        fetch.start()
    fetches[0].wait()
    rot = rotation(gen_ref[...])
    rot_high, rot_low = split(rot)
    rot_ref[0] = rot_high
    rot_ref[1] = rot_low
    coarse_ref[...] = jnp.clip(rot, -F8_MAX, F8_MAX).astype(F8)
    fetches[1].wait()
    fetches[2].wait()

    def run(k, states, done):
        for s in range(done, SEG):
            out = []
            for g in range(CHUNKS):
                t = g * per + per - 1 - k * SEG - s
                moved = step_rows(states[g] * d_ref[pl.ds(t, 1), :], width, rot_ref, coarse_ref)
                out.append(
                    jnp.concatenate([moved[:width], moved[width:] + f_ref[t].astype(F32)], axis=0)
                )
            states = out
        for g in range(CHUNKS):
            raw_ref[g * marks + marks - 1 - k] = states[g]

    first = []
    for g in range(CHUNKS):
        end = (g + 1) * per
        column = d_ref[end - 8 : end, :].T[:, 7:8]
        first.append(jnp.concatenate([rot * column, f_ref[end - 1].astype(F32)], axis=0))
    run(0, first, 1)

    def more(k, _):
        run(k, [raw_ref[g * marks + marks - k] for g in range(CHUNKS)], 0)
        return 0

    lax.fori_loop(1, marks, more, 0)
    maps = [raw_ref[g * marks] for g in range(CHUNKS)]
    while len(maps) > 1:
        maps = [compose(maps[i + 1], maps[i], width) for i in range(0, len(maps), 2)]
    map_ref[...] = maps[0]


def marks_kernel(raw_ref, in_hbm, _, zh_ref, zl_ref, zu_ref, flip_ref, __, in_ref, sem):
    fetch = pltpu.make_async_copy(in_hbm, in_ref, sem)
    fetch.start()
    count, rows, width = raw_ref.shape
    marks = count // CHUNKS
    suffix = None
    for g in range(CHUNKS - 1, -1, -1):
        for j in range((g + 1) * marks - 1, g * marks - 1, -1):
            full = raw_ref[j]
            if suffix is not None:
                full = compose(suffix, full, width)
            high, low = split(full[:width])
            zh_ref[j] = high
            zl_ref[j] = low
            zu_ref[j] = full[width:]
        suffix = full
    fetch.wait()
    segs = in_ref.shape[0] // SEG
    for s in range(SEG):
        block = jnp.concatenate([in_ref[m * SEG + s] for m in range(segs)], axis=0)
        flip_ref[s] = block.T


def early(bit):
    return (lax.axis_index("tm") & bit) == 0


def core_half(ref):
    half = ref.shape[0] // 2
    return ref[pl.ds(pl.multiple_of((lax.axis_index("tm") & 1) * half, half), half), :]


def place_halves(mine, other, out_ref):
    half = mine.shape[0]
    start = pl.multiple_of((lax.axis_index("tm") & 1) * half, half)
    out_ref[pl.ds(start, half), :] = mine
    out_ref[pl.ds(pl.multiple_of(half - start, half), half), :] = other


def ordered(bit, own_ref, other_ref, out_ref):
    width = own_ref.shape[1]
    first = early(bit)

    @pl.when(first)
    def _():
        out_ref[...] = compose(other_ref[...], own_ref[...], width)

    @pl.when(jnp.logical_not(first))
    def _():
        out_ref[...] = compose(own_ref[...], other_ref[...], width)


def pair_kernel(own_ref, other_ref, out_ref, half_ref):
    ordered(1, own_ref, other_ref, out_ref)
    half_ref[...] = core_half(out_ref)


def position(low_bit, count):
    return (lax.axis_index("tm") // low_bit) % count


def group_maps(own_ref, halves, maps):
    maps[0] = own_ref[...]
    for mask in range(1, maps.shape[0]):
        place_halves(halves[2 * mask - 2][...], halves[2 * mask - 1][...], maps.at[mask])


def top_kernel(low_bit, own_ref, vec_ref, *rest):
    halves, (out_ref, maps) = rest[:-2], rest[-2:]
    group_maps(own_ref, halves, maps)
    count, _, width = maps.shape
    here = position(low_bit, count)
    vec = vec_ref[...]
    final = maps[(count // 2 - 1) ^ here]
    for at in range(count // 2 - 2, -1, -1):
        final = compose(final, maps[at ^ here], width)
    for at in range(count - 1, count // 2 - 1, -1):
        vec = apply(vec, maps[at ^ here], width)
    out_ref[...] = apply(vec, final, width)


def total_kernel(low_bit, own_ref, *rest):
    halves, (out_ref, half_ref, maps) = rest[:-3], rest[-3:]
    group_maps(own_ref, halves, maps)
    count, _, width = maps.shape
    here = position(low_bit, count)
    acc = maps[(count - 1) ^ here]
    for at in range(count - 2, -1, -1):
        acc = compose(acc, maps[at ^ here], width)
    out_ref[...] = acc
    half_ref[...] = core_half(out_ref)


def later_kernel(low_bit, later_ref, *rest):
    halves, (out_ref, maps) = rest[:-2], rest[-2:]
    count, _, width = maps.shape
    for mask in range(1, count):
        place_halves(halves[2 * mask - 2][...], halves[2 * mask - 1][...], maps.at[mask])
    here = position(low_bit, count)
    maps[0] = later_ref[...]
    out_ref[...] = maps[jnp.where(here == count - 1, 0, (count - 1) ^ here)]
    for at in range(count - 2, -1, -1):

        @pl.when(at >= here)
        def _():
            out_ref[...] = compose(out_ref[...], maps[at ^ here], width)


def first_later_kernel(bit, other_ref, out_ref):
    rows, width = other_ref.shape
    first = early(bit)

    @pl.when(first)
    def _():
        out_ref[...] = other_ref[...]

    @pl.when(jnp.logical_not(first))
    def _():
        out_ref[...] = (
            lax.broadcasted_iota(jnp.int32, (rows, width), 0) == lax.broadcasted_iota(jnp.int32, (rows, width), 1)
        ).astype(F32)


def sweep_kernel(
    bit, end_ref, got_ref, later_ref, zh_ref, zl_ref, zu_ref,
    rot_ref, d_ref, f_ref, flip_ref,
    adj_hbm, keep_ref, give_ref, cur, low_ref, sems,
):
    count, width = zh_ref.shape[0], zh_ref.shape[1]
    cols = end_ref.shape[0]
    v = jnp.where(early(bit), got_ref[...], end_ref[...])
    v = apply(v, later_ref[...], width)
    v_high, v_low = split(v)
    v_both = jnp.concatenate([v_high, v_low], axis=0)

    def send(at):
        return pltpu.make_async_copy(low_ref.at[at], adj_hbm.at[:, at], sems.at[at])

    for j in range(count):
        both = mm(v_both, zh_ref[j])
        z = both[:cols] + both[cols:] + mm(v_high, zl_ref[j]) + zu_ref[j]
        if j > 0:
            cur[j - 1] = z
        low_ref[0, j] = z.astype(BF16)
    cur[count - 1] = v
    send(0).start()
    grad = mm(flip_ref[0], low_ref[0].reshape(count * cols, width))
    pack = 4
    for s in range(SEG - 1):
        at = SEG - 1 - s
        for p in range(0, count, pack):
            scaled = jnp.concatenate(
                [cur[m] * d_ref[m * SEG + at : m * SEG + at + 1, :] for m in range(p, p + pack)], axis=0
            )
            out = mm3(scaled, rot_ref[0], rot_ref[1])
            for m in range(p, p + pack):
                value = out[(m - p) * cols : (m - p + 1) * cols] + f_ref[m * SEG + at].astype(F32)
                cur[m] = value
                low_ref[at, m] = value.astype(BF16)
        send(at).start()
        grad = grad + mm(flip_ref[at], low_ref[at].reshape(count * cols, width))
    grad = grad.T
    half = width // 2
    first = early(1)
    keep_ref[...] = jnp.where(first, grad[:half], grad[half:])
    give_ref[...] = jnp.where(first, grad[half:], grad[:half])
    for at in range(SEG):
        send(at).wait()


def halve_kernel(bit, keep_ref, got_ref, mine_ref, give_ref):
    total = keep_ref[...] + got_ref[...]
    half = total.shape[0] // 2
    first = early(bit)
    mine_ref[...] = jnp.where(first, total[:half], total[half:])
    give_ref[...] = jnp.where(first, total[half:], total[:half])


def join_kernel(bit, own_ref, far_ref, core_ref, both_ref, out_hbm, sems):
    rows = own_ref.shape[0]
    place = lax.axis_index("tm")
    low, high = place & 1, (place // bit) & 1
    sends = []
    for i, (ref, a, b) in enumerate(
        (
            (own_ref, low, high),
            (far_ref, low, 1 - high),
            (core_ref, 1 - low, high),
            (both_ref, 1 - low, 1 - high),
        )
    ):
        start = pl.multiple_of((2 * a + b) * rows, rows)
        sends.append(pltpu.make_async_copy(ref, out_hbm.at[pl.ds(start, rows), :], sems.at[i]))
    for send in sends:
        send.start()
    for send in sends:
        send.wait()


VM = pltpu.VMEM


def call(kernel, name, out, *args, where=None, scratch=(), flops=0, data=0, alias=None):
    where = where or {}
    ins = [pl.BlockSpec(memory_space=pl.ANY if i in where else VM) for i in range(len(args))]
    args = [pltpu.with_memory_space_constraint(a, pltpu.HBM if i in where else VM) for i, a in enumerate(args)]
    outs = tuple(
        pl.BlockSpec(memory_space=pl.ANY if isinstance(o, jax.ShapeDtypeStruct) else VM) for o in out
    )
    return pl.pallas_call(
        kernel,
        out_shape=tuple(out),
        in_specs=ins,
        out_specs=outs,
        scratch_shapes=list(scratch),
        input_output_aliases=alias or {},
        compiler_params=pltpu.CompilerParams(vmem_limit_bytes=VMEM_LIMIT),
        cost_estimate=pl.CostEstimate(flops=flops, bytes_accessed=data, transcendentals=0),
        name=name,
    )(*args)


def build(gen, derivs, force):
    steps, width = derivs.shape
    cols = force.shape[1]
    rows = width + cols
    return call(
        build_kernel,
        "build",
        (
            VM((rows, width), F32),
            VM((steps // SEG, rows, width), F32),
            VM((2, width, width), BF16),
            VM(derivs.shape, F32),
            VM(force.shape, BF16),
        ),
        gen,
        derivs,
        force,
        where={0, 1, 2},
        scratch=[VM(gen.shape, F32), VM(gen.shape, F8), pltpu.SemaphoreType.DMA((3,))],
        flops=6 * steps * rows * width * width,
    )


def mark_maps(raw, ins, through):
    count, rows, width = raw.shape
    steps, cols, feats = ins.shape
    return call(
        marks_kernel,
        "marks",
        (
            VM((count, width, width), BF16),
            VM((count, width, width), BF16),
            VM((count, rows - width, width), F32),
            VM((SEG, feats, steps // SEG * cols), BF16),
            VM(through.shape, F32),
        ),
        raw,
        ins,
        through,
        alias={2: 4},
        where={1},
        scratch=[VM(ins.shape, BF16), pltpu.SemaphoreType.DMA],
        flops=6 * count * rows * width * width,
        data=15_000_000,
    )


def sweep(entering, later, zh, zl, zu, rot, derivs, force, flipped):
    steps, cols, width = force.shape
    feats = flipped.shape[1]
    segs = steps // SEG
    adj, keep, give = call(
        functools.partial(sweep_kernel, lax.axis_size("tm") // 2),
        "sweep",
        (
            shape((segs, SEG, cols, width), BF16),
            VM((width // 2, feats), F32),
            VM((width // 2, feats), F32),
        ),
        *entering, later, zh, zl, zu, rot, derivs, force, flipped,
        scratch=[
            VM((segs, cols, width), F32),
            VM((SEG, segs, cols, width), BF16),
            pltpu.SemaphoreType.DMA((SEG,)),
        ],
        flops=8 * steps * cols * width * width,
    )
    return adj.reshape(steps, cols, width), keep, give


def shape(dims, kind=F32):
    return jax.ShapeDtypeStruct(dims, kind)


def swap(x, bit):
    n = lax.axis_size("tm")
    return lax.ppermute(x, "tm", [(i, i ^ bit) for i in range(n)])


def incoming(own, end, aside):
    n = lax.axis_size("tm")
    rows, width = own.shape
    flops = 6 * rows * width * width
    vec = VM(end.shape, F32)
    whole = VM(own.shape, F32)
    half = VM((rows // 2, width), F32)
    other = swap(own, 1)
    total, piece = call(pair_kernel, "pair", (whole, half), own, other, flops=flops)
    (later,) = call(functools.partial(first_later_kernel, 1), "later", (whole,), other)
    bit = 2
    while bit < n // 2:
        count = 4 if 4 * bit <= n // 2 else 2
        mine = [swap(piece, mask * bit) for mask in range(1, count)]
        if bit == 2:
            *marks, mine[0] = aside(mine[0])
        halves = [x for got in mine for x in (got, swap(got, 1))]
        maps = [VM((count, rows, width), F32)]
        if count * bit < n // 2:
            total, piece = call(
                functools.partial(total_kernel, bit), "total", (whole, half), total, *halves,
                scratch=maps, flops=count * flops,
            )
        else:
            (top,) = call(
                functools.partial(top_kernel, bit), "top", (vec,), total, end, *halves,
                scratch=maps, flops=count * flops // 5,
            )
        (later,) = call(
            functools.partial(later_kernel, bit), "later", (whole,), later, *halves,
            scratch=maps, flops=count * flops,
        )
        bit *= count
    return marks, (end, swap(top, n // 2)), later


def all_sum(keep, give):
    n = lax.axis_size("tm")
    near = 2
    quarter = VM((keep.shape[0] // 2, keep.shape[1]), F32)
    x, give = call(functools.partial(halve_kernel, near), "halve", (quarter, quarter), keep, swap(give, 1))
    x = x + swap(give, near)
    bit = 2 * near
    while bit < n:
        count = 4 if 4 * bit <= n else 2
        others = [swap(x, mask * bit) for mask in range(1, count)]
        x = sum(others, x)
        bit *= count
    far = swap(x, near)
    core = swap(x, 1)
    both = swap(far, 1)
    (out,) = call(
        functools.partial(join_kernel, near), "join", (shape((4 * x.shape[0], x.shape[1])),), x, far, core, both,
        scratch=[pltpu.SemaphoreType.DMA((4,))],
    )
    return out


def body(generator, derivs, forcing, inputs, terminal):
    force = jnp.transpose(forcing, (0, 2, 1))
    ins = jnp.transpose(inputs, (0, 2, 1))
    end = terminal.T
    own, raw, rot, derivs, force = build(generator, derivs, force)
    (zh, zl, zu, flipped), entering, later = incoming(own, end, functools.partial(mark_maps, raw, ins))
    adj, keep, give = sweep(entering, later, zh, zl, zu, rot, derivs, force, flipped)
    return jnp.transpose(adj, (0, 2, 1)), all_sum(keep, give)


def solution(mesh):
    in_specs = (
        P(),
        P(("groups", "tm"), None),
        P(("groups", "tm"), None, None),
        P(("groups", "tm"), None, None),
        P("groups", None),
    )
    out_specs = (P(("groups", "tm"), None, None), P("groups", None))
    return jax.shard_map(body, mesh=mesh, in_specs=in_specs, out_specs=out_specs, check_vma=False)
```

```python
import functools
import math

import jax
import jax.numpy as jnp
from jax import lax
from jax.experimental import pallas as pl
from jax.experimental.pallas import tpu as pltpu
from jax.sharding import PartitionSpec as P

F32 = jnp.float32
BF16 = jnp.bfloat16
F8 = jnp.float8_e4m3fn
LIFT = 1024.0
F8_MAX = 448.0
VMEM_LIMIT = 24 * 1024 * 1024
CHUNKS = 4
SEG = 8


def mm(a, b):
    return jnp.dot(a, b, preferred_element_type=F32)


def split(x):
    high = x.astype(BF16)
    low = (x - high.astype(F32)).astype(BF16)
    return high, low


def mm3(a, b_high, b_low):
    a_high, a_low = split(a)
    return mm(a_high, b_high) + mm(a_low, b_high) + mm(a_high, b_low)


def rotation(gen):
    n = gen.shape[0]
    skew = gen - gen.T
    ident = (
        lax.broadcasted_iota(jnp.int32, (n, n), 0) == lax.broadcasted_iota(jnp.int32, (n, n), 1)
    ).astype(F32)
    c = [1.0 / math.factorial(k) for k in range(13)]
    halves = split(skew)
    s2 = mm3(skew, *halves)
    s3 = mm3(s2, *halves)
    s4 = mm3(s2, *split(s2))
    top = c[8] * ident + c[9] * skew + c[10] * s2 + c[11] * s3 + c[12] * s4
    mid = c[4] * ident + c[5] * skew + c[6] * s2 + c[7] * s3
    bottom = ident + skew + c[2] * s2 + c[3] * s3
    inner = mid + mm3(s4, *split(top))
    return bottom + mm3(s4, *split(inner))


def step_rows(x, width, rot_ref, coarse_ref):
    rows = x.shape[0]
    high = x.astype(BF16)
    low = x - high.astype(F32)
    both = mm(jnp.concatenate([high, low[width:].astype(BF16)], axis=0), rot_ref[0])
    fine = mm(high, rot_ref[1])
    lifted = jnp.clip(low[:width] * LIFT, -F8_MAX, F8_MAX).astype(F8)
    small = mm(lifted, coarse_ref[...]) * (1.0 / LIFT)
    return jnp.concatenate(
        [both[:width] + fine[:width] + small, both[width:rows] + fine[width:] + both[rows:]], axis=0
    )


def compose(rows_in, through, width):
    high, low = split(through[:width])
    out = mm3(rows_in, high, low)
    return jnp.concatenate([out[:width], out[width:] + through[width:]], axis=0)


def apply(vec, through, width):
    high, low = split(through[:width])
    return mm3(vec, high, low) + through[width:]


def build_kernel(gen_hbm, d_hbm, f_hbm, map_ref, raw_ref, rot_ref, d_ref, f_ref, gen_ref, coarse_ref, sems):
    steps, width = d_ref.shape
    per = steps // CHUNKS
    marks = per // SEG
    fetches = [
        pltpu.make_async_copy(far, here, sems.at[i])
        for i, (far, here) in enumerate(((gen_hbm, gen_ref), (d_hbm, d_ref), (f_hbm, f_ref)))
    ]
    for fetch in fetches:
        fetch.start()
    fetches[0].wait()
    rot = rotation(gen_ref[...])
    rot_high, rot_low = split(rot)
    rot_ref[0] = rot_high
    rot_ref[1] = rot_low
    coarse_ref[...] = jnp.clip(rot, -F8_MAX, F8_MAX).astype(F8)
    fetches[1].wait()
    fetches[2].wait()

    def run(k, states, done):
        for s in range(done, SEG):
            out = []
            for g in range(CHUNKS):
                t = g * per + per - 1 - k * SEG - s
                moved = step_rows(states[g] * d_ref[pl.ds(t, 1), :], width, rot_ref, coarse_ref)
                out.append(
                    jnp.concatenate([moved[:width], moved[width:] + f_ref[t].astype(F32)], axis=0)
                )
            states = out
        for g in range(CHUNKS):
            raw_ref[g * marks + marks - 1 - k] = states[g]

    first = []
    for g in range(CHUNKS):
        end = (g + 1) * per
        column = d_ref[end - 8 : end, :].T[:, 7:8]
        first.append(jnp.concatenate([rot * column, f_ref[end - 1].astype(F32)], axis=0))
    run(0, first, 1)

    def more(k, _):
        run(k, [raw_ref[g * marks + marks - k] for g in range(CHUNKS)], 0)
        return 0

    lax.fori_loop(1, marks, more, 0)
    maps = [raw_ref[g * marks] for g in range(CHUNKS)]
    while len(maps) > 1:
        maps = [compose(maps[i + 1], maps[i], width) for i in range(0, len(maps), 2)]
    map_ref[...] = maps[0]


def marks_kernel(raw_ref, in_hbm, own_ref, other_ref, _, zh_ref, zl_ref, zu_ref, flip_ref, pair_ref, __, in_ref, sem):
    fetch = pltpu.make_async_copy(in_hbm, in_ref, sem)
    fetch.start()
    ordered(1, own_ref, other_ref, pair_ref)
    count, rows, width = raw_ref.shape
    marks = count // CHUNKS
    suffix = None
    for g in range(CHUNKS - 1, -1, -1):
        for j in range((g + 1) * marks - 1, g * marks - 1, -1):
            full = raw_ref[j]
            if suffix is not None:
                full = compose(suffix, full, width)
            high, low = split(full[:width])
            zh_ref[j] = high
            zl_ref[j] = low
            zu_ref[j] = full[width:]
        suffix = full
    fetch.wait()
    segs = in_ref.shape[0] // SEG
    for s in range(SEG):
        block = jnp.concatenate([in_ref[m * SEG + s] for m in range(segs)], axis=0)
        flip_ref[s] = block.T


def early(bit):
    return (lax.axis_index("tm") & bit) == 0


def core_half(ref):
    half = ref.shape[0] // 2
    return ref[pl.ds(pl.multiple_of((lax.axis_index("tm") & 1) * half, half), half), :]


def place_halves(mine, other, out_ref):
    half = mine.shape[0]
    start = pl.multiple_of((lax.axis_index("tm") & 1) * half, half)
    out_ref[pl.ds(start, half), :] = mine
    out_ref[pl.ds(pl.multiple_of(half - start, half), half), :] = other


def ordered(bit, own_ref, other_ref, out_ref):
    width = own_ref.shape[1]
    first = early(bit)

    @pl.when(first)
    def _():
        out_ref[...] = compose(other_ref[...], own_ref[...], width)

    @pl.when(jnp.logical_not(first))
    def _():
        out_ref[...] = compose(own_ref[...], other_ref[...], width)


def pair_kernel(own_ref, other_ref, half_ref):
    half, width = half_ref.shape
    first = early(1)

    @pl.when(first)
    def _():
        half_ref[...] = mm3(other_ref[:half], *split(own_ref[:width]))

    @pl.when(jnp.logical_not(first))
    def _():
        out = mm3(own_ref[half:], *split(other_ref[:width]))
        edge = width - half
        half_ref[...] = jnp.concatenate([out[:edge], out[edge:] + other_ref[width:]], axis=0)


def position(low_bit, count):
    return (lax.axis_index("tm") // low_bit) % count


def group_maps(own_ref, halves, maps):
    maps[0] = own_ref[...]
    for mask in range(1, maps.shape[0]):
        place_halves(halves[2 * mask - 2][...], halves[2 * mask - 1][...], maps.at[mask])


def top_kernel(low_bit, own_ref, vec_ref, *rest):
    halves, (out_ref, maps) = rest[:-2], rest[-2:]
    group_maps(own_ref, halves, maps)
    count, _, width = maps.shape
    here = position(low_bit, count)
    vec = vec_ref[...]
    final = maps[(count // 2 - 1) ^ here]
    for at in range(count // 2 - 2, -1, -1):
        final = compose(final, maps[at ^ here], width)
    for at in range(count - 1, count // 2 - 1, -1):
        vec = apply(vec, maps[at ^ here], width)
    out_ref[...] = apply(vec, final, width)


def total_kernel(low_bit, own_ref, *rest):
    halves, (out_ref, half_ref, maps) = rest[:-3], rest[-3:]
    group_maps(own_ref, halves, maps)
    count, _, width = maps.shape
    here = position(low_bit, count)
    acc = maps[(count - 1) ^ here]
    for at in range(count - 2, -1, -1):
        acc = compose(acc, maps[at ^ here], width)
    out_ref[...] = acc
    half_ref[...] = core_half(out_ref)


def later_kernel(low_bit, later_ref, *rest):
    halves, (out_ref, maps) = rest[:-2], rest[-2:]
    count, _, width = maps.shape
    for mask in range(1, count):
        place_halves(halves[2 * mask - 2][...], halves[2 * mask - 1][...], maps.at[mask])
    here = position(low_bit, count)
    maps[0] = later_ref[...]
    out_ref[...] = maps[jnp.where(here == count - 1, 0, (count - 1) ^ here)]
    for at in range(count - 2, -1, -1):

        @pl.when(at >= here)
        def _():
            out_ref[...] = compose(out_ref[...], maps[at ^ here], width)


def first_later_kernel(bit, other_ref, out_ref):
    rows, width = other_ref.shape
    first = early(bit)

    @pl.when(first)
    def _():
        out_ref[...] = other_ref[...]

    @pl.when(jnp.logical_not(first))
    def _():
        out_ref[...] = (
            lax.broadcasted_iota(jnp.int32, (rows, width), 0) == lax.broadcasted_iota(jnp.int32, (rows, width), 1)
        ).astype(F32)


def sweep_kernel(
    bit, end_ref, got_ref, later_ref, zh_ref, zl_ref, zu_ref,
    rot_ref, d_ref, f_ref, flip_ref,
    adj_hbm, keep_ref, give_ref, cur, low_ref, sems,
):
    count, width = zh_ref.shape[0], zh_ref.shape[1]
    cols = end_ref.shape[0]
    v = jnp.where(early(bit), got_ref[...], end_ref[...])
    v = apply(v, later_ref[...], width)
    v_high, v_low = split(v)
    v_both = jnp.concatenate([v_high, v_low], axis=0)

    def send(at):
        return pltpu.make_async_copy(low_ref.at[at], adj_hbm.at[:, at], sems.at[at])

    pack = 4

    def tail(p):
        part = pl.ds(p, pack)
        return pltpu.make_async_copy(low_ref.at[1, part], adj_hbm.at[part, 1], sems.at[SEG + p // pack])

    for j in range(count):
        both = mm(v_both, zh_ref[j])
        z = both[:cols] + both[cols:] + mm(v_high, zl_ref[j]) + zu_ref[j]
        if j > 0:
            cur[j - 1] = z
        low_ref[0, j] = z.astype(BF16)
    cur[count - 1] = v
    send(0).start()
    grad = mm(flip_ref[0], low_ref[0].reshape(count * cols, width))
    for s in range(SEG - 1):
        at = SEG - 1 - s
        for p in range(0, count, pack):
            scaled = jnp.concatenate(
                [cur[m] * d_ref[m * SEG + at : m * SEG + at + 1, :] for m in range(p, p + pack)], axis=0
            )
            out = mm3(scaled, rot_ref[0], rot_ref[1])
            for m in range(p, p + pack):
                value = out[(m - p) * cols : (m - p + 1) * cols] + f_ref[m * SEG + at].astype(F32)
                cur[m] = value
                low_ref[at, m] = value.astype(BF16)
            if at == 1:
                tail(p).start()
        if at > 1:
            send(at).start()
        grad = grad + mm(flip_ref[at], low_ref[at].reshape(count * cols, width))
    grad = grad.T
    half = width // 2
    first = early(1)
    keep_ref[...] = jnp.where(first, grad[:half], grad[half:])
    give_ref[...] = jnp.where(first, grad[half:], grad[:half])
    for at in range(SEG):
        if at != 1:
            send(at).wait()
    for p in range(0, count, pack):
        tail(p).wait()


def halve_kernel(bit, keep_ref, got_ref, mine_ref, give_ref):
    total = keep_ref[...] + got_ref[...]
    half = total.shape[0] // 2
    first = early(bit)
    mine_ref[...] = jnp.where(first, total[:half], total[half:])
    give_ref[...] = jnp.where(first, total[half:], total[:half])


def join_kernel(bit, own_ref, far_ref, core_ref, both_ref, out_hbm, sems):
    rows = own_ref.shape[0]
    place = lax.axis_index("tm")
    low, high = place & 1, (place // bit) & 1
    sends = []
    for i, (ref, a, b) in enumerate(
        (
            (own_ref, low, high),
            (far_ref, low, 1 - high),
            (core_ref, 1 - low, high),
            (both_ref, 1 - low, 1 - high),
        )
    ):
        start = pl.multiple_of((2 * a + b) * rows, rows)
        sends.append(pltpu.make_async_copy(ref, out_hbm.at[pl.ds(start, rows), :], sems.at[i]))
    for send in sends:
        send.start()
    for send in sends:
        send.wait()


VM = pltpu.VMEM


def call(kernel, name, out, *args, where=None, scratch=(), flops=0, data=0, alias=None):
    where = where or {}
    ins = [pl.BlockSpec(memory_space=pl.ANY if i in where else VM) for i in range(len(args))]
    args = [pltpu.with_memory_space_constraint(a, pltpu.HBM if i in where else VM) for i, a in enumerate(args)]
    outs = tuple(
        pl.BlockSpec(memory_space=pl.ANY if isinstance(o, jax.ShapeDtypeStruct) else VM) for o in out
    )
    return pl.pallas_call(
        kernel,
        out_shape=tuple(out),
        in_specs=ins,
        out_specs=outs,
        scratch_shapes=list(scratch),
        input_output_aliases=alias or {},
        compiler_params=pltpu.CompilerParams(vmem_limit_bytes=VMEM_LIMIT),
        cost_estimate=pl.CostEstimate(flops=flops, bytes_accessed=data, transcendentals=0),
        name=name,
    )(*args)


def build(gen, derivs, force):
    steps, width = derivs.shape
    cols = force.shape[1]
    rows = width + cols
    return call(
        build_kernel,
        "build",
        (
            VM((rows, width), F32),
            VM((steps // SEG, rows, width), F32),
            VM((2, width, width), BF16),
            VM(derivs.shape, F32),
            VM(force.shape, BF16),
        ),
        gen,
        derivs,
        force,
        where={0, 1, 2},
        scratch=[VM(gen.shape, F32), VM(gen.shape, F8), pltpu.SemaphoreType.DMA((3,))],
        flops=6 * steps * rows * width * width,
    )


def mark_maps(raw, ins, own, other, through):
    count, rows, width = raw.shape
    steps, cols, feats = ins.shape
    return call(
        marks_kernel,
        "marks",
        (
            VM((count, width, width), BF16),
            VM((count, width, width), BF16),
            VM((count, rows - width, width), F32),
            VM((SEG, feats, steps // SEG * cols), BF16),
            VM((rows, width), F32),
            VM(through.shape, F32),
        ),
        raw,
        ins,
        own,
        other,
        through,
        alias={4: 5},
        where={1},
        scratch=[VM(ins.shape, BF16), pltpu.SemaphoreType.DMA],
        flops=6 * count * rows * width * width,
        data=15_000_000,
    )


def sweep(entering, later, zh, zl, zu, rot, derivs, force, flipped):
    steps, cols, width = force.shape
    feats = flipped.shape[1]
    segs = steps // SEG
    adj, keep, give = call(
        functools.partial(sweep_kernel, lax.axis_size("tm") // 2),
        "sweep",
        (
            shape((segs, SEG, cols, width), BF16),
            VM((width // 2, feats), F32),
            VM((width // 2, feats), F32),
        ),
        *entering, later, zh, zl, zu, rot, derivs, force, flipped,
        scratch=[
            VM((segs, cols, width), F32),
            VM((SEG, segs, cols, width), BF16),
            pltpu.SemaphoreType.DMA((SEG + segs // 4,)),
        ],
        flops=8 * steps * cols * width * width,
    )
    return adj.reshape(steps, cols, width), keep, give


def shape(dims, kind=F32):
    return jax.ShapeDtypeStruct(dims, kind)


def swap(x, bit):
    n = lax.axis_size("tm")
    return lax.ppermute(x, "tm", [(i, i ^ bit) for i in range(n)])


def incoming(own, end, aside):
    n = lax.axis_size("tm")
    rows, width = own.shape
    flops = 6 * rows * width * width
    vec = VM(end.shape, F32)
    whole = VM(own.shape, F32)
    half = VM((rows // 2, width), F32)
    other = swap(own, 1)
    (piece,) = call(pair_kernel, "pair", (half,), own, other, flops=flops // 2)
    (later,) = call(functools.partial(first_later_kernel, 1), "later", (whole,), other)
    bit = 2
    while bit < n // 2:
        count = 4 if 4 * bit <= n // 2 else 2
        mine = [swap(piece, mask * bit) for mask in range(1, count)]
        if bit == 2:
            *marks, total, mine[0] = aside(own, other, mine[0])
        halves = [x for got in mine for x in (got, swap(got, 1))]
        maps = [VM((count, rows, width), F32)]
        if count * bit < n // 2:
            total, piece = call(
                functools.partial(total_kernel, bit), "total", (whole, half), total, *halves,
                scratch=maps, flops=count * flops,
            )
        else:
            (top,) = call(
                functools.partial(top_kernel, bit), "top", (vec,), total, end, *halves,
                scratch=maps, flops=count * flops // 5,
            )
        (later,) = call(
            functools.partial(later_kernel, bit), "later", (whole,), later, *halves,
            scratch=maps, flops=count * flops,
        )
        bit *= count
    return marks, (end, swap(top, n // 2)), later


def all_sum(keep, give):
    n = lax.axis_size("tm")
    near = 2
    quarter = VM((keep.shape[0] // 2, keep.shape[1]), F32)
    x, give = call(functools.partial(halve_kernel, near), "halve", (quarter, quarter), keep, swap(give, 1))
    x = x + swap(give, near)
    bit = 2 * near
    while bit < n:
        count = 4 if 4 * bit <= n else 2
        others = [swap(x, mask * bit) for mask in range(count - 1, 0, -1)]
        x = sum(others, x)
        bit *= count
    far = swap(x, near)
    core = swap(x, 1)
    both = swap(far, 1)
    (out,) = call(
        functools.partial(join_kernel, near), "join", (shape((4 * x.shape[0], x.shape[1])),), x, far, core, both,
        scratch=[pltpu.SemaphoreType.DMA((4,))],
    )
    return out


def body(generator, derivs, forcing, inputs, terminal):
    force = jnp.transpose(forcing, (0, 2, 1))
    ins = jnp.transpose(inputs, (0, 2, 1))
    end = terminal.T
    own, raw, rot, derivs, force = build(generator, derivs, force)
    (zh, zl, zu, flipped), entering, later = incoming(own, end, functools.partial(mark_maps, raw, ins))
    adj, keep, give = sweep(entering, later, zh, zl, zu, rot, derivs, force, flipped)
    return jnp.transpose(adj, (0, 2, 1)), all_sum(keep, give)


def solution(mesh):
    in_specs = (
        P(),
        P(("groups", "tm"), None),
        P(("groups", "tm"), None, None),
        P(("groups", "tm"), None, None),
        P("groups", None),
    )
    out_specs = (P(("groups", "tm"), None, None), P("groups", None))
    return jax.shard_map(body, mesh=mesh, in_specs=in_specs, out_specs=out_specs, check_vma=False)
```

```python
import functools
import math

import jax
import jax.numpy as jnp
from jax import lax
from jax.experimental import pallas as pl
from jax.experimental.pallas import tpu as pltpu
from jax.sharding import PartitionSpec as P

F32 = jnp.float32
BF16 = jnp.bfloat16
F8 = jnp.float8_e4m3fn
LIFT = 1024.0
F8_MAX = 448.0
VMEM_LIMIT = 24 * 1024 * 1024
CHUNKS = 4
SEG = 8


def mm(a, b):
    return jnp.dot(a, b, preferred_element_type=F32)


def split(x):
    high = x.astype(BF16)
    low = (x - high.astype(F32)).astype(BF16)
    return high, low


def mm3(a, b_high, b_low):
    a_high, a_low = split(a)
    return mm(a_high, b_high) + mm(a_low, b_high) + mm(a_high, b_low)


def rotation(gen):
    n = gen.shape[0]
    skew = gen - gen.T
    ident = (
        lax.broadcasted_iota(jnp.int32, (n, n), 0) == lax.broadcasted_iota(jnp.int32, (n, n), 1)
    ).astype(F32)
    c = [1.0 / math.factorial(k) for k in range(13)]
    halves = split(skew)
    s2 = mm3(skew, *halves)
    s3 = mm3(s2, *halves)
    s4 = mm3(s2, *split(s2))
    top = c[8] * ident + c[9] * skew + c[10] * s2 + c[11] * s3 + c[12] * s4
    mid = c[4] * ident + c[5] * skew + c[6] * s2 + c[7] * s3
    bottom = ident + skew + c[2] * s2 + c[3] * s3
    inner = mid + mm3(s4, *split(top))
    return bottom + mm3(s4, *split(inner))


def step_rows(x, width, rot_ref, coarse_ref):
    rows = x.shape[0]
    high = x.astype(BF16)
    low = x - high.astype(F32)
    both = mm(jnp.concatenate([high, low[width:].astype(BF16)], axis=0), rot_ref[0])
    fine = mm(high, rot_ref[1])
    lifted = jnp.clip(low[:width] * LIFT, -F8_MAX, F8_MAX).astype(F8)
    small = mm(lifted, coarse_ref[...]) * (1.0 / LIFT)
    return jnp.concatenate(
        [both[:width] + fine[:width] + small, both[width:rows] + fine[width:] + both[rows:]], axis=0
    )


def compose(rows_in, through, width):
    high, low = split(through[:width])
    out = mm3(rows_in, high, low)
    return jnp.concatenate([out[:width], out[width:] + through[width:]], axis=0)


def apply(vec, through, width):
    high, low = split(through[:width])
    return mm3(vec, high, low) + through[width:]


def build_kernel(gen_hbm, d_hbm, f_hbm, map_ref, raw_ref, rot_ref, d_ref, f_ref, gen_ref, coarse_ref, sems):
    steps, width = d_ref.shape
    per = steps // CHUNKS
    marks = per // SEG
    fetches = [
        pltpu.make_async_copy(far, here, sems.at[i])
        for i, (far, here) in enumerate(((gen_hbm, gen_ref), (d_hbm, d_ref), (f_hbm, f_ref)))
    ]
    for fetch in fetches:
        fetch.start()
    fetches[0].wait()
    rot = rotation(gen_ref[...])
    rot_high, rot_low = split(rot)
    rot_ref[0] = rot_high
    rot_ref[1] = rot_low
    coarse_ref[...] = jnp.clip(rot, -F8_MAX, F8_MAX).astype(F8)
    fetches[1].wait()
    fetches[2].wait()

    def run(k, states, done):
        for s in range(done, SEG):
            out = []
            for g in range(CHUNKS):
                t = g * per + per - 1 - k * SEG - s
                moved = step_rows(states[g] * d_ref[pl.ds(t, 1), :], width, rot_ref, coarse_ref)
                out.append(
                    jnp.concatenate([moved[:width], moved[width:] + f_ref[t].astype(F32)], axis=0)
                )
            states = out
        for g in range(CHUNKS):
            raw_ref[g * marks + marks - 1 - k] = states[g]

    first = []
    for g in range(CHUNKS):
        end = (g + 1) * per
        column = d_ref[end - 8 : end, :].T[:, 7:8]
        first.append(jnp.concatenate([rot * column, f_ref[end - 1].astype(F32)], axis=0))
    run(0, first, 1)

    def more(k, _):
        run(k, [raw_ref[g * marks + marks - k] for g in range(CHUNKS)], 0)
        return 0

    lax.fori_loop(1, marks, more, 0)
    maps = [raw_ref[g * marks] for g in range(CHUNKS)]
    while len(maps) > 1:
        maps = [compose(maps[i + 1], maps[i], width) for i in range(0, len(maps), 2)]
    map_ref[...] = maps[0]


def marks_kernel(raw_ref, in_hbm, own_ref, other_ref, _, zh_ref, zl_ref, zu_ref, flip_ref, pair_ref, __, in_ref, sem):
    fetch = pltpu.make_async_copy(in_hbm, in_ref, sem)
    fetch.start()
    ordered(1, own_ref, other_ref, pair_ref)
    count, rows, width = raw_ref.shape
    marks = count // CHUNKS
    suffix = None
    for g in range(CHUNKS - 1, -1, -1):
        for j in range((g + 1) * marks - 1, g * marks - 1, -1):
            full = raw_ref[j]
            if suffix is not None:
                full = compose(suffix, full, width)
            high, low = split(full[:width])
            zh_ref[j] = high
            zl_ref[j] = low
            zu_ref[j] = full[width:]
        suffix = full
    fetch.wait()
    segs = in_ref.shape[0] // SEG
    for s in range(SEG):
        block = jnp.concatenate([in_ref[m * SEG + s] for m in range(segs)], axis=0)
        flip_ref[s] = block.T


def early(bit):
    return (lax.axis_index("tm") & bit) == 0


def core_half(ref):
    half = ref.shape[0] // 2
    return ref[pl.ds(pl.multiple_of((lax.axis_index("tm") & 1) * half, half), half), :]


def place_halves(mine, other, out_ref):
    half = mine.shape[0]
    start = pl.multiple_of((lax.axis_index("tm") & 1) * half, half)
    out_ref[pl.ds(start, half), :] = mine
    out_ref[pl.ds(pl.multiple_of(half - start, half), half), :] = other


def ordered(bit, own_ref, other_ref, out_ref):
    width = own_ref.shape[1]
    first = early(bit)

    @pl.when(first)
    def _():
        out_ref[...] = compose(other_ref[...], own_ref[...], width)

    @pl.when(jnp.logical_not(first))
    def _():
        out_ref[...] = compose(own_ref[...], other_ref[...], width)


def pair_kernel(own_ref, other_ref, half_ref):
    half, width = half_ref.shape
    first = early(1)

    @pl.when(first)
    def _():
        half_ref[...] = mm3(other_ref[:half], *split(own_ref[:width]))

    @pl.when(jnp.logical_not(first))
    def _():
        out = mm3(own_ref[half:], *split(other_ref[:width]))
        edge = width - half
        half_ref[...] = jnp.concatenate([out[:edge], out[edge:] + other_ref[width:]], axis=0)


def position(low_bit, count):
    return (lax.axis_index("tm") // low_bit) % count


def group_maps(own_ref, halves, maps):
    maps[0] = own_ref[...]
    for mask in range(1, maps.shape[0]):
        place_halves(halves[2 * mask - 2][...], halves[2 * mask - 1][...], maps.at[mask])


def top_kernel(low_bit, own_ref, vec_ref, *rest):
    halves, (out_ref, maps) = rest[:-2], rest[-2:]
    group_maps(own_ref, halves, maps)
    count, _, width = maps.shape
    here = position(low_bit, count)
    vec = vec_ref[...]
    final = maps[(count // 2 - 1) ^ here]
    for at in range(count // 2 - 2, -1, -1):
        final = compose(final, maps[at ^ here], width)
    for at in range(count - 1, count // 2 - 1, -1):
        vec = apply(vec, maps[at ^ here], width)
    out_ref[...] = apply(vec, final, width)


def total_kernel(low_bit, own_ref, *rest):
    halves, (out_ref, half_ref, maps) = rest[:-3], rest[-3:]
    group_maps(own_ref, halves, maps)
    count, _, width = maps.shape
    here = position(low_bit, count)
    acc = maps[(count - 1) ^ here]
    for at in range(count - 2, -1, -1):
        acc = compose(acc, maps[at ^ here], width)
    out_ref[...] = acc
    half_ref[...] = core_half(out_ref)


def later_kernel(low_bit, later_ref, *rest):
    halves, (out_ref, maps) = rest[:-2], rest[-2:]
    count, _, width = maps.shape
    for mask in range(1, count):
        place_halves(halves[2 * mask - 2][...], halves[2 * mask - 1][...], maps.at[mask])
    here = position(low_bit, count)
    maps[0] = later_ref[...]
    out_ref[...] = maps[jnp.where(here == count - 1, 0, (count - 1) ^ here)]
    for at in range(count - 2, -1, -1):

        @pl.when(at >= here)
        def _():
            out_ref[...] = compose(out_ref[...], maps[at ^ here], width)


def first_later_kernel(bit, other_ref, out_ref):
    rows, width = other_ref.shape
    first = early(bit)

    @pl.when(first)
    def _():
        out_ref[...] = other_ref[...]

    @pl.when(jnp.logical_not(first))
    def _():
        out_ref[...] = (
            lax.broadcasted_iota(jnp.int32, (rows, width), 0) == lax.broadcasted_iota(jnp.int32, (rows, width), 1)
        ).astype(F32)


def shift_kernel(later_ref, zh_ref, zl_ref, zu_ref, outh_ref, outl_ref, outu_ref):
    width = later_ref.shape[1]
    for j in range(zh_ref.shape[0]):
        out = mm3(later_ref[...], zh_ref[j], zl_ref[j])
        outu_ref[j] = out[width:] + zu_ref[j]
        high, low = split(out[:width])
        outh_ref[j] = high
        outl_ref[j] = low


def sweep_kernel(
    bit, end_ref, got_ref, later_ref, zh_ref, zl_ref, zu_ref,
    rot_ref, d_ref, f_ref, flip_ref,
    adj_hbm, keep_ref, give_ref, cur, low_ref, sems,
):
    count, width = zh_ref.shape[0], zh_ref.shape[1]
    cols = end_ref.shape[0]
    v = jnp.where(early(bit), got_ref[...], end_ref[...])
    start = apply(v, later_ref[...], width)
    v_high, v_low = split(v)
    v_both = jnp.concatenate([v_high, v_low], axis=0)

    def send(at):
        return pltpu.make_async_copy(low_ref.at[at], adj_hbm.at[:, at], sems.at[at])

    pack = 4

    def tail(p):
        part = pl.ds(p, pack)
        return pltpu.make_async_copy(low_ref.at[1, part], adj_hbm.at[part, 1], sems.at[SEG + p // pack])

    for j in range(count):
        both = mm(v_both, zh_ref[j])
        z = both[:cols] + both[cols:] + mm(v_high, zl_ref[j]) + zu_ref[j]
        if j > 0:
            cur[j - 1] = z
        low_ref[0, j] = z.astype(BF16)
    cur[count - 1] = start
    send(0).start()
    grad = mm(flip_ref[0], low_ref[0].reshape(count * cols, width))
    for s in range(SEG - 1):
        at = SEG - 1 - s
        for p in range(0, count, pack):
            scaled = jnp.concatenate(
                [cur[m] * d_ref[m * SEG + at : m * SEG + at + 1, :] for m in range(p, p + pack)], axis=0
            )
            out = mm3(scaled, rot_ref[0], rot_ref[1])
            for m in range(p, p + pack):
                value = out[(m - p) * cols : (m - p + 1) * cols] + f_ref[m * SEG + at].astype(F32)
                cur[m] = value
                low_ref[at, m] = value.astype(BF16)
            if at == 1:
                tail(p).start()
        if at > 1:
            send(at).start()
        grad = grad + mm(flip_ref[at], low_ref[at].reshape(count * cols, width))
    grad = grad.T
    half = width // 2
    first = early(1)
    keep_ref[...] = jnp.where(first, grad[:half], grad[half:])
    give_ref[...] = jnp.where(first, grad[half:], grad[:half])
    for at in range(SEG):
        if at != 1:
            send(at).wait()
    for p in range(0, count, pack):
        tail(p).wait()


def halve_kernel(bit, keep_ref, got_ref, mine_ref, give_ref):
    total = keep_ref[...] + got_ref[...]
    half = total.shape[0] // 2
    first = early(bit)
    mine_ref[...] = jnp.where(first, total[:half], total[half:])
    give_ref[...] = jnp.where(first, total[half:], total[:half])


def join_kernel(bit, own_ref, far_ref, core_ref, both_ref, out_hbm, sems):
    rows = own_ref.shape[0]
    place = lax.axis_index("tm")
    low, high = place & 1, (place // bit) & 1
    sends = []
    for i, (ref, a, b) in enumerate(
        (
            (own_ref, low, high),
            (far_ref, low, 1 - high),
            (core_ref, 1 - low, high),
            (both_ref, 1 - low, 1 - high),
        )
    ):
        start = pl.multiple_of((2 * a + b) * rows, rows)
        sends.append(pltpu.make_async_copy(ref, out_hbm.at[pl.ds(start, rows), :], sems.at[i]))
    for send in sends:
        send.start()
    for send in sends:
        send.wait()


VM = pltpu.VMEM


def call(kernel, name, out, *args, where=None, scratch=(), flops=0, data=0, alias=None):
    where = where or {}
    ins = [pl.BlockSpec(memory_space=pl.ANY if i in where else VM) for i in range(len(args))]
    args = [pltpu.with_memory_space_constraint(a, pltpu.HBM if i in where else VM) for i, a in enumerate(args)]
    outs = tuple(
        pl.BlockSpec(memory_space=pl.ANY if isinstance(o, jax.ShapeDtypeStruct) else VM) for o in out
    )
    return pl.pallas_call(
        kernel,
        out_shape=tuple(out),
        in_specs=ins,
        out_specs=outs,
        scratch_shapes=list(scratch),
        input_output_aliases=alias or {},
        compiler_params=pltpu.CompilerParams(vmem_limit_bytes=VMEM_LIMIT),
        cost_estimate=pl.CostEstimate(flops=flops, bytes_accessed=data, transcendentals=0),
        name=name,
    )(*args)


def build(gen, derivs, force):
    steps, width = derivs.shape
    cols = force.shape[1]
    rows = width + cols
    return call(
        build_kernel,
        "build",
        (
            VM((rows, width), F32),
            VM((steps // SEG, rows, width), F32),
            VM((2, width, width), BF16),
            VM(derivs.shape, F32),
            VM(force.shape, BF16),
        ),
        gen,
        derivs,
        force,
        where={0, 1, 2},
        scratch=[VM(gen.shape, F32), VM(gen.shape, F8), pltpu.SemaphoreType.DMA((3,))],
        flops=6 * steps * rows * width * width,
    )


def mark_maps(raw, ins, own, other, through):
    count, rows, width = raw.shape
    steps, cols, feats = ins.shape
    return call(
        marks_kernel,
        "marks",
        (
            VM((count, width, width), BF16),
            VM((count, width, width), BF16),
            VM((count, rows - width, width), F32),
            VM((SEG, feats, steps // SEG * cols), BF16),
            VM((rows, width), F32),
            VM(through.shape, F32),
        ),
        raw,
        ins,
        own,
        other,
        through,
        alias={4: 5},
        where={1},
        scratch=[VM(ins.shape, BF16), pltpu.SemaphoreType.DMA],
        flops=6 * count * rows * width * width,
        data=15_000_000,
    )


def shift(later, zh, zl, zu):
    count, width, _ = zh.shape
    return call(
        shift_kernel,
        "shift",
        (VM(zh.shape, BF16), VM(zl.shape, BF16), VM(zu.shape, F32)),
        later, zh, zl, zu,
        flops=6 * count * later.shape[0] * width * width,
    )


def sweep(entering, later, zh, zl, zu, rot, derivs, force, flipped):
    steps, cols, width = force.shape
    feats = flipped.shape[1]
    segs = steps // SEG
    adj, keep, give = call(
        functools.partial(sweep_kernel, lax.axis_size("tm") // 2),
        "sweep",
        (
            shape((segs, SEG, cols, width), BF16),
            VM((width // 2, feats), F32),
            VM((width // 2, feats), F32),
        ),
        *entering, later, zh, zl, zu, rot, derivs, force, flipped,
        scratch=[
            VM((segs, cols, width), F32),
            VM((SEG, segs, cols, width), BF16),
            pltpu.SemaphoreType.DMA((SEG + segs // 4,)),
        ],
        flops=8 * steps * cols * width * width,
    )
    return adj.reshape(steps, cols, width), keep, give


def shape(dims, kind=F32):
    return jax.ShapeDtypeStruct(dims, kind)


def swap(x, bit):
    n = lax.axis_size("tm")
    return lax.ppermute(x, "tm", [(i, i ^ bit) for i in range(n)])


def incoming(own, end, aside):
    n = lax.axis_size("tm")
    rows, width = own.shape
    flops = 6 * rows * width * width
    vec = VM(end.shape, F32)
    whole = VM(own.shape, F32)
    half = VM((rows // 2, width), F32)
    other = swap(own, 1)
    (piece,) = call(pair_kernel, "pair", (half,), own, other, flops=flops // 2)
    (later,) = call(functools.partial(first_later_kernel, 1), "later", (whole,), other)
    bit = 2
    while bit < n // 2:
        count = 4 if 4 * bit <= n // 2 else 2
        mine = [swap(piece, mask * bit) for mask in range(1, count)]
        if bit == 2:
            *marks, total, mine[0] = aside(own, other, mine[0])
        halves = [x for got in mine for x in (got, swap(got, 1))]
        maps = [VM((count, rows, width), F32)]
        if count * bit < n // 2:
            total, piece = call(
                functools.partial(total_kernel, bit), "total", (whole, half), total, *halves,
                scratch=maps, flops=count * flops,
            )
        else:
            (top,) = call(
                functools.partial(top_kernel, bit), "top", (vec,), total, end, *halves,
                scratch=maps, flops=count * flops // 5,
            )
        (later,) = call(
            functools.partial(later_kernel, bit), "later", (whole,), later, *halves,
            scratch=maps, flops=count * flops,
        )
        bit *= count
    return marks, (end, swap(top, n // 2)), later


def all_sum(keep, give):
    n = lax.axis_size("tm")
    near = 2
    quarter = VM((keep.shape[0] // 2, keep.shape[1]), F32)
    x, give = call(functools.partial(halve_kernel, near), "halve", (quarter, quarter), keep, swap(give, 1))
    x = x + swap(give, near)
    bit = 2 * near
    while bit < n:
        count = 4 if 4 * bit <= n else 2
        others = [swap(x, mask * bit) for mask in range(1, count)]
        x = sum(others, x)
        bit *= count
    far = swap(x, near)
    core = swap(x, 1)
    both = swap(far, 1)
    (out,) = call(
        functools.partial(join_kernel, near), "join", (shape((4 * x.shape[0], x.shape[1])),), x, far, core, both,
        scratch=[pltpu.SemaphoreType.DMA((4,))],
    )
    return out


def body(generator, derivs, forcing, inputs, terminal):
    force = jnp.transpose(forcing, (0, 2, 1))
    ins = jnp.transpose(inputs, (0, 2, 1))
    end = terminal.T
    own, raw, rot, derivs, force = build(generator, derivs, force)
    (zh, zl, zu, flipped), entering, later = incoming(own, end, functools.partial(mark_maps, raw, ins))
    zh, zl, zu = shift(later, zh, zl, zu)
    adj, keep, give = sweep(entering, later, zh, zl, zu, rot, derivs, force, flipped)
    return jnp.transpose(adj, (0, 2, 1)), all_sum(keep, give)


def solution(mesh):
    in_specs = (
        P(),
        P(("groups", "tm"), None),
        P(("groups", "tm"), None, None),
        P(("groups", "tm"), None, None),
        P("groups", None),
    )
    out_specs = (P(("groups", "tm"), None, None), P("groups", None))
    return jax.shard_map(body, mesh=mesh, in_specs=in_specs, out_specs=out_specs, check_vma=False)
```
